32 devices in a mesh: wave: 4 (over y, x), pix: 8 (over z, core).
Axes of the slice: x: 2, y: 2, z: 4, core: 2. Of those that a mesh axis runs over, the one named last changes fastest.
Arguments:
- raw_spectra: bfloat16 [2, 2, 16384, 2048], P(None, None, 'wave', 'pix'), may hold values from -6 to 6
- background: float32 [16384], P('wave'), may hold values from -6 to 6
- dispersion: float32 [16384], P('wave'), may hold values from -3.140625 to 3.140625
- propagator: bfloat16 [2, 2048, 2048], P(None, None, 'pix'), may hold values from -0.09375 to 0.09375
Outputs:
- image: float32 [2, 2, 16384, 2048], P(None, None, ('wave', 'pix'))
The draws below stay inside these ranges and needn't reach their ends.
All inputs are finite; a program needn't handle non-finite values.
Results may differ from the reference program's by a relative error of at most 0.0029.
Values may be sent and summed in bfloat16 or wider, within the bound.
No kernel may reach another device: no remote copies, remote signals or barrier semaphores. Data moves between devices by JAX's collectives and lax.ppermute only.
A program may use at most 192 MiB of HBM per device.

```python
import jax
import jax.numpy as jnp

K = 16384
PIX = 2048
ROWS = 2


def shard_levels(stream_key, extent, split, low, top_value):
    level, own = 1.0, jax.random.fold_in(stream_key, 6)
    for position, blocks in split:
        heights = jnp.exp(jax.random.uniform(jax.random.fold_in(own, position), (blocks,), jnp.float32, low / len(split), top_value / len(split)))
        level = level * jnp.repeat(heights, extent[position] // blocks).reshape([-1 if axis == position else 1 for axis in range(len(extent))])
    return level


def noise(key, dims, width, most, pieces=(), dtype=jnp.bfloat16):
    result = jax.random.normal(key, dims, jnp.float32) * width
    if len(pieces) > 0:
        result = shard_levels(key, dims, pieces, -0.22, 0.18) * result
    return jnp.clip(result, min=-most, max=most).astype(dtype)


def setup_inputs(seed: int = 0) -> dict:
    arg_keys = jax.random.split(jax.random.key(seed), 5)
    return {
        "raw_spectra": noise(arg_keys[0], (2, ROWS, K, PIX), 1.0, 6.0, ((2, 4), (3, 8))),
        "background": noise(arg_keys[1], (K,), 1.0, 6.0, ((0, 4),), jnp.float32),
        "dispersion": jnp.clip(jax.random.uniform(arg_keys[2], (K,), jnp.float32, -3.140625, 3.140625), -3.140625, 3.140625),
        "propagator": noise(arg_keys[3], (2, PIX, PIX), (2 * PIX) ** -0.5, 0.09375, ((2, 8),)),
    }


def reference(raw_spectra, background, dispersion, propagator):
    real_part = raw_spectra[0].astype(jnp.float32) - background[None, :, None]
    imag_part = raw_spectra[1].astype(jnp.float32)
    cosine = jnp.cos(dispersion)[None, :, None]
    sine_part = jnp.sin(dispersion)[None, :, None]
    turned = real_part * cosine - imag_part * sine_part + 1j * (real_part * sine_part + imag_part * cosine)
    transform = jnp.fft.fft(turned, axis=1) / jnp.sqrt(jnp.float32(K))
    depth_real = jnp.real(transform).astype(jnp.bfloat16)
    depth_imag = jnp.imag(transform).astype(jnp.bfloat16)
    prop_real = propagator[0]
    prop_imag = propagator[1]
    image_real = jnp.dot(depth_real, prop_real, preferred_element_type=jnp.float32) - jnp.dot(depth_imag, prop_imag, preferred_element_type=jnp.float32)
    image_imag = jnp.dot(depth_real, prop_imag, preferred_element_type=jnp.float32) + jnp.dot(depth_imag, prop_real, preferred_element_type=jnp.float32)
    return jnp.stack((image_real, image_imag))
```

```python
import functools
import math

import jax
import jax.numpy as jnp
import numpy as np
from jax import lax
from jax.experimental import pallas as pl
from jax.experimental.pallas import tpu as pltpu
from jax.sharding import PartitionSpec as P

CHUNK = 16
VMEM_BYTES = 56 * 1024 * 1024


def unit_roots(rows, columns, modulus):
    product = np.outer(np.arange(rows), np.arange(columns)) % modulus
    angle = -2.0 * np.pi / modulus * product
    return np.cos(angle), np.sin(angle)


def split(value):
    high = value.astype(jnp.bfloat16)
    return high, (value - high.astype(jnp.float32)).astype(jnp.bfloat16)


def transform_kernel(
    steps, x_ref, phase_ref, small_ref, turn_ref, fine_ref, out_ref, data, high, low, part
):
    step = pl.program_id(0)
    k1_count, pixels = data.shape[2], data.shape[3]

    @pl.when(step < steps)
    def _():
        for c in range(2):
            block = x_ref[:, c].reshape(k1_count, CHUNK, pixels).astype(jnp.float32)
            data[c] = jnp.swapaxes(block, 0, 1).astype(jnp.bfloat16)
        for i in range(CHUNK):
            turn_real = turn_ref[0, 0, :, i : i + 1]
            turn_imag = turn_ref[1, 0, :, i : i + 1]
            cosine = phase_ref[0, i : i + 1, :]
            sine = phase_ref[1, i : i + 1, :]
            background = phase_ref[2, i : i + 1, :]
            small_real = small_ref[0] * turn_real - small_ref[1] * turn_imag
            small_imag = small_ref[0] * turn_imag + small_ref[1] * turn_real
            real = small_real * cosine - small_imag * sine
            imag = small_real * sine + small_imag * cosine
            base_real = jnp.sum(real * background, axis=1, keepdims=True)
            base_imag = jnp.sum(imag * background, axis=1, keepdims=True)
            real_high, real_low = split(real)
            imag_high, imag_low = split(imag)
            matrix = jnp.concatenate((real_high, imag_high, real_low, imag_low), axis=0)
            columns = jnp.concatenate((data[0, i], data[1, i]), axis=1)
            both = jnp.dot(matrix, columns, preferred_element_type=jnp.float32)
            half = 2 * k1_count
            both = both[:half] + both[half:]
            by_real, by_imag = both[:k1_count], both[k1_count:]
            part[0, i] = by_real[:, :pixels] - by_imag[:, pixels:] - base_real
            part[1, i] = by_real[:, pixels:] + by_imag[:, :pixels] - base_imag
        at = pl.ds(pl.multiple_of(step * CHUNK, CHUNK), CHUNK)
        for c in range(2):
            turned = jnp.swapaxes(part[c], 0, 1)
            turned_high, turned_low = split(turned)
            high[c, :, at, :] = turned_high
            low[c, :, at, :] = turned_low

    @pl.when(step >= steps)
    def _():
        first = (step - steps) * CHUNK
        for i in range(CHUNK):
            at = first + i
            columns = jnp.concatenate((high[0, at], high[1, at]), axis=1)
            rest = jnp.concatenate((low[0, at], low[1, at]), axis=1)
            both = jnp.dot(fine_ref[...], columns, preferred_element_type=jnp.float32)
            half = both.shape[0] // 2
            both = (
                both[:half]
                + both[half:]
                + jnp.dot(fine_ref[:half], rest, preferred_element_type=jnp.float32)
            )
            by_real, by_imag = both[: half // 2], both[half // 2 :]
            part[0, i] = by_real[:, :pixels] - by_imag[:, pixels:]
            part[1, i] = by_real[:, pixels:] + by_imag[:, :pixels]
        for c in range(2):
            turned = jnp.swapaxes(part[c], 0, 1).astype(jnp.bfloat16)
            out_ref[:, c] = turned.reshape(out_ref.shape[:1] + out_ref.shape[2:])


def depth_transform(blocks, phases, devices):
    wave_count, _, k1_part, k0_count, pixels = blocks.shape
    k1_count = wave_count * k1_part
    length = k1_count * k0_count
    z0_count, z1_count = k1_count, k0_count
    steps = k0_count // CHUNK
    small = np.stack(unit_roots(z0_count, k1_count, k1_count)).astype(np.float32)
    turn = np.stack(unit_roots(z0_count, k0_count, length)).astype(np.float32)
    turn = turn.reshape(2, z0_count, steps, CHUNK).transpose(0, 2, 1, 3)
    fine = np.concatenate(unit_roots(z1_count, k0_count, k0_count), axis=0) / math.sqrt(length)
    fine_high = fine.astype(jnp.bfloat16)
    fine_low = (fine - fine_high.astype(np.float64)).astype(jnp.bfloat16)
    fine = np.concatenate((fine_high, fine_low), axis=0)
    out_shape = (devices, 2, z1_count // devices, z0_count, pixels)
    return pl.pallas_call(
        functools.partial(transform_kernel, steps),
        out_shape=jax.ShapeDtypeStruct(out_shape, jnp.bfloat16),
        grid=(2 * steps,),
        in_specs=[
            pl.BlockSpec(
                (wave_count, 2, k1_part, CHUNK, pixels),
                lambda i: (0, 0, 0, jnp.minimum(i, steps - 1), 0),
            ),
            pl.BlockSpec((3, CHUNK, k1_count), lambda i: (0, jnp.minimum(i, steps - 1), 0)),
            pl.BlockSpec(small.shape, lambda i: (0, 0, 0)),
            pl.BlockSpec(
                (2, 1, z0_count, CHUNK), lambda i: (0, jnp.minimum(i, steps - 1), 0, 0)
            ),
            pl.BlockSpec(fine.shape, lambda i: (0, 0)),
        ],
        out_specs=pl.BlockSpec(
            out_shape[:3] + (CHUNK, pixels), lambda i: (0, 0, 0, jnp.maximum(i - steps, 0), 0)
        ),
        scratch_shapes=[
            pltpu.VMEM((2, CHUNK, k1_count, pixels), jnp.bfloat16),
            pltpu.VMEM((2, z0_count, k0_count, pixels), jnp.bfloat16),
            pltpu.VMEM((2, z0_count, k0_count, pixels), jnp.bfloat16),
            pltpu.VMEM((2, CHUNK, z0_count, pixels), jnp.float32),
        ],
        compiler_params=pltpu.CompilerParams(vmem_limit_bytes=VMEM_BYTES),
        cost_estimate=pl.CostEstimate(
            flops=2 * 5 * 4 * 128 * length * pixels,
            bytes_accessed=8 * length * pixels,
            transcendentals=0,
        ),
    )(blocks, phases, jnp.asarray(small), jnp.asarray(turn), jnp.asarray(fine))


def refocus_kernel(row_count, pix_count, tile, depth_ref, prop_ref, out_ref):
    senders = depth_ref.shape[0]
    pieces = senders // (row_count * pix_count)
    depths = depth_ref.shape[2]
    for r in range(row_count):
        for t in range(depths // tile):
            rows = pl.ds(t * tile, tile)
            parts = []
            for c in range(2):
                parts.append(
                    jnp.concatenate(
                        [
                            depth_ref[(r * pieces + h) * pix_count + p, c, rows, :]
                            for p in range(pix_count)
                            for h in range(pieces)
                        ],
                        axis=1,
                    )
                )
            dot = functools.partial(jnp.dot, preferred_element_type=jnp.float32)
            real, imag = parts
            out_ref[0, r, rows, :] = dot(real, prop_ref[0, 0]) - dot(imag, prop_ref[0, 1])
            out_ref[1, r, rows, :] = dot(real, prop_ref[0, 1]) + dot(imag, prop_ref[0, 0])


def refocus(depth, propagator, row_count):
    pix_count, _, span, width = propagator.shape
    depths = depth.shape[2]
    tile = min(256, depths)
    return pl.pallas_call(
        functools.partial(refocus_kernel, row_count, pix_count, tile),
        out_shape=jax.ShapeDtypeStruct(
            (2, row_count, depths, pix_count * width), jnp.float32
        ),
        grid=(pix_count,),
        in_specs=[
            pl.BlockSpec(depth.shape, lambda q: (0, 0, 0, 0)),
            pl.BlockSpec((1, 2, span, width), lambda q: (q, 0, 0, 0)),
        ],
        out_specs=pl.BlockSpec((2, row_count, depths, width), lambda q: (0, 0, 0, q)),
        compiler_params=pltpu.CompilerParams(vmem_limit_bytes=VMEM_BYTES),
        cost_estimate=pl.CostEstimate(
            flops=8 * row_count * depths * span * pix_count * width,
            bytes_accessed=32 * 1024 * 1024,
            transcendentals=0,
        ),
    )(depth, propagator)


def on_device(raw_spectra, background, dispersion, propagator):
    _, row_count, wave_span, pix_local = raw_spectra.shape
    wave_count = lax.axis_size("wave")
    pix_count = lax.axis_size("pix")
    devices = wave_count * pix_count
    pieces = wave_count // row_count
    pixels = pix_local // pieces
    k0_count = 128
    k1_part = wave_span // k0_count

    columns = lax.all_gather(propagator, "pix", axis=0, tiled=False)
    phases = jnp.stack((jnp.cos(dispersion), jnp.sin(dispersion), background))
    phases = lax.all_gather(phases.reshape(3, k1_part, k0_count), "wave", axis=1, tiled=True)
    phases = jnp.swapaxes(phases, 1, 2)

    outgoing = raw_spectra.reshape(2, row_count, wave_span, pieces, pixels)
    outgoing = jnp.transpose(outgoing, (1, 3, 0, 2, 4)).reshape(
        wave_count, 2, wave_span, pixels
    )
    blocks = lax.all_to_all(outgoing, "wave", split_axis=0, concat_axis=0, tiled=True)
    blocks = blocks.reshape(wave_count, 2, k1_part, k0_count, pixels)
    depth = depth_transform(blocks, phases, devices)
    depth = depth.reshape(devices, 2, -1, pixels)
    depth = lax.all_to_all(depth, ("wave", "pix"), split_axis=0, concat_axis=0, tiled=True)
    return refocus(depth, columns, row_count)


def solution(mesh):
    in_specs = (P(None, None, "wave", "pix"), P("wave"), P("wave"), P(None, None, "pix"))
    out_specs = P(None, None, ("wave", "pix"), None)
    return jax.shard_map(
        on_device, mesh=mesh, in_specs=in_specs, out_specs=out_specs, check_vma=False
    )
```

```python
import functools
import math

import jax
import jax.numpy as jnp
import numpy as np
from jax import lax
from jax.experimental import pallas as pl
from jax.experimental.pallas import tpu as pltpu
from jax.sharding import PartitionSpec as P

CHUNK = 16
SEND_CHUNKS = 2
DEPTH_CHUNKS = 2
VMEM_BYTES = 56 * 1024 * 1024


def unit_roots(rows, columns, modulus):
    product = np.outer(np.arange(rows), np.arange(columns)) % modulus
    angle = -2.0 * np.pi / modulus * product
    return np.cos(angle), np.sin(angle)


def split(value):
    high = value.astype(jnp.bfloat16)
    return high, (value - high.astype(jnp.float32)).astype(jnp.bfloat16)


def pack_kernel(raw_ref, out_ref):
    pixels = out_ref.shape[4]
    for h in range(out_ref.shape[0]):
        out_ref[h] = raw_ref[:, 0, :, :, h * pixels : (h + 1) * pixels]


def pack(raw, wave_count, chunk, width):
    _, row_count, k1_part, _, pix_local = raw.shape
    pieces = wave_count // row_count
    pixels = pix_local // pieces
    split_k1 = min(8, k1_part)
    return pl.pallas_call(
        pack_kernel,
        out_shape=jax.ShapeDtypeStruct((wave_count, 2, k1_part, width, pixels), raw.dtype),
        grid=(row_count, k1_part // split_k1),
        in_specs=[
            pl.BlockSpec((2, 1, split_k1, width, pix_local), lambda r, k: (0, r, k, chunk, 0))
        ],
        out_specs=pl.BlockSpec(
            (pieces, 2, split_k1, width, pixels), lambda r, k: (r, 0, k, 0, 0)
        ),
        compiler_params=pltpu.CompilerParams(vmem_limit_bytes=VMEM_BYTES),
        cost_estimate=pl.CostEstimate(
            flops=0,
            bytes_accessed=8 * row_count * k1_part * width * pix_local,
            transcendentals=0,
        ),
    )(raw)


def coarse_kernel(x_ref, phase_ref, small_ref, turn_ref, high_ref, low_ref, data, part):
    k1_count, pixels = data.shape[2], data.shape[3]
    for c in range(2):
        block = x_ref[:, c].reshape(k1_count, CHUNK, pixels).astype(jnp.float32)
        data[c] = jnp.swapaxes(block, 0, 1).astype(jnp.bfloat16)
    for i in range(CHUNK):
        turn_real = turn_ref[0, 0, :, i : i + 1]
        turn_imag = turn_ref[1, 0, :, i : i + 1]
        cosine = phase_ref[0, i : i + 1, :]
        sine = phase_ref[1, i : i + 1, :]
        background = phase_ref[2, i : i + 1, :]
        small_real = small_ref[0] * turn_real - small_ref[1] * turn_imag
        small_imag = small_ref[0] * turn_imag + small_ref[1] * turn_real
        real = small_real * cosine - small_imag * sine
        imag = small_real * sine + small_imag * cosine
        base_real = jnp.sum(real * background, axis=1, keepdims=True)
        base_imag = jnp.sum(imag * background, axis=1, keepdims=True)
        real_high, real_low = split(real)
        imag_high, imag_low = split(imag)
        matrix = jnp.concatenate((real_high, imag_high, real_low, imag_low), axis=0)
        columns = jnp.concatenate((data[0, i], data[1, i]), axis=1)
        both = jnp.dot(matrix, columns, preferred_element_type=jnp.float32)
        half = 2 * k1_count
        both = both[:half] + both[half:]
        by_real, by_imag = both[:k1_count], both[k1_count:]
        part[0, i] = by_real[:, :pixels] - by_imag[:, pixels:] - base_real
        part[1, i] = by_real[:, pixels:] + by_imag[:, :pixels] - base_imag
    for c in range(2):
        turned_high, turned_low = split(jnp.swapaxes(part[c], 0, 1))
        high_ref[c] = turned_high
        low_ref[c] = turned_low


def coarse_stage(blocks, phases, chunk):
    wave_count, _, k1_part, width, pixels = blocks.shape
    k1_count, k0_count = wave_count * k1_part, phases.shape[1]
    length = k1_count * k0_count
    steps = width // CHUNK
    small = np.stack(unit_roots(k1_count, k1_count, k1_count)).astype(np.float32)
    turn = np.stack(unit_roots(k1_count, k0_count, length)).astype(np.float32)
    turn = turn.reshape(2, k1_count, k0_count // CHUNK, CHUNK).transpose(0, 2, 1, 3)
    out_shape = jax.ShapeDtypeStruct((2, k1_count, width, pixels), jnp.bfloat16)
    out_spec = pl.BlockSpec((2, k1_count, CHUNK, pixels), lambda i: (0, 0, i, 0))
    return pl.pallas_call(
        coarse_kernel,
        out_shape=(out_shape, out_shape),
        grid=(steps,),
        in_specs=[
            pl.BlockSpec((wave_count, 2, k1_part, CHUNK, pixels), lambda i: (0, 0, 0, i, 0)),
            pl.BlockSpec((3, CHUNK, k1_count), lambda i: (0, chunk * steps + i, 0)),
            pl.BlockSpec(small.shape, lambda i: (0, 0, 0)),
            pl.BlockSpec((2, 1, k1_count, CHUNK), lambda i: (0, chunk * steps + i, 0, 0)),
        ],
        out_specs=(out_spec, out_spec),
        scratch_shapes=[
            pltpu.VMEM((2, CHUNK, k1_count, pixels), jnp.bfloat16),
            pltpu.VMEM((2, CHUNK, k1_count, pixels), jnp.float32),
        ],
        compiler_params=pltpu.CompilerParams(vmem_limit_bytes=VMEM_BYTES),
        cost_estimate=pl.CostEstimate(
            flops=16 * k1_count * k1_count * width * pixels * 2,
            bytes_accessed=12 * k1_count * width * pixels,
            transcendentals=0,
        ),
    )(blocks, phases, jnp.asarray(small), jnp.asarray(turn))


def fine_kernel(chunks, *refs):
    highs, lows = refs[:chunks], refs[chunks : 2 * chunks]
    fine_ref, out_ref, part = refs[2 * chunks :]
    pixels = out_ref.shape[4]

    def gathered(sources, i):
        return jnp.concatenate(
            [jnp.concatenate([ref[c, i] for ref in sources], axis=0) for c in range(2)], axis=1
        )

    for i in range(CHUNK):
        both = jnp.dot(fine_ref[...], gathered(highs, i), preferred_element_type=jnp.float32)
        half = both.shape[0] // 2
        both = (
            both[:half]
            + both[half:]
            + jnp.dot(fine_ref[:half], gathered(lows, i), preferred_element_type=jnp.float32)
        )
        by_real, by_imag = both[: half // 2], both[half // 2 :]
        part[0, i] = by_real[:, :pixels] - by_imag[:, pixels:]
        part[1, i] = by_real[:, pixels:] + by_imag[:, :pixels]
    for c in range(2):
        turned = jnp.swapaxes(part[c], 0, 1).astype(jnp.bfloat16)
        out_ref[:, c] = turned.reshape(out_ref.shape[:1] + out_ref.shape[2:])


def fine_stage(highs, lows, devices, chunk, width):
    _, z0_count, k0_part, pixels = highs[0].shape
    chunks = len(highs)
    k0_count = chunks * k0_part
    steps = width // CHUNK
    length = k0_count * z0_count
    fine = np.concatenate(unit_roots(k0_count, k0_count, k0_count), axis=0) / math.sqrt(length)
    fine_high = fine.astype(jnp.bfloat16)
    fine_low = (fine - fine_high.astype(np.float64)).astype(jnp.bfloat16)
    fine = np.concatenate((fine_high, fine_low), axis=0)
    out_shape = (devices, 2, k0_count // devices, width, pixels)
    in_spec = pl.BlockSpec(
        (2, CHUNK, k0_part, pixels), lambda i: (0, chunk * steps + i, 0, 0)
    )
    return pl.pallas_call(
        functools.partial(fine_kernel, chunks),
        out_shape=jax.ShapeDtypeStruct(out_shape, jnp.bfloat16),
        grid=(steps,),
        in_specs=[in_spec] * (2 * chunks) + [pl.BlockSpec(fine.shape, lambda i: (0, 0))],
        out_specs=pl.BlockSpec(out_shape[:3] + (CHUNK, pixels), lambda i: (0, 0, 0, i, 0)),
        scratch_shapes=[pltpu.VMEM((2, CHUNK, k0_count, pixels), jnp.float32)],
        compiler_params=pltpu.CompilerParams(vmem_limit_bytes=VMEM_BYTES),
        cost_estimate=pl.CostEstimate(
            flops=24 * k0_count * k0_count * width * pixels * 2,
            bytes_accessed=12 * k0_count * width * pixels,
            transcendentals=0,
        ),
    )(*highs, *lows, jnp.asarray(fine))


def refocus_kernel(row_count, pix_count, depth_ref, prop_ref, *rest):
    out_ref = rest[-1]
    senders, _, z1_part, width, pixels = depth_ref.shape
    pieces = senders // (row_count * pix_count)
    dot = functools.partial(jnp.dot, preferred_element_type=jnp.float32)
    for r in range(row_count):
        real, imag = [
            jnp.concatenate(
                [
                    depth_ref[(r * pieces + h) * pix_count + p, c].reshape(z1_part * width, pixels)
                    for p in range(pix_count)
                    for h in range(pieces)
                ],
                axis=1,
            )
            for c in range(2)
        ]
        shape = (z1_part, width, out_ref.shape[4])
        image_real = dot(real, prop_ref[0, 0]) - dot(imag, prop_ref[0, 1])
        out_ref[0, r] = image_real.reshape(shape)
        image_imag = dot(real, prop_ref[0, 1]) + dot(imag, prop_ref[0, 0])
        out_ref[1, r] = image_imag.reshape(shape)


def refocus(depth, propagator, row_count, chunk, chunks, image):
    pix_count, _, span, columns = propagator.shape
    _, _, z1_part, width, _ = depth.shape
    out_shape = (2, row_count, z1_part, width * chunks, pix_count * columns)
    earlier = () if image is None else (image,)
    return pl.pallas_call(
        functools.partial(refocus_kernel, row_count, pix_count),
        out_shape=jax.ShapeDtypeStruct(out_shape, jnp.float32),
        grid=(pix_count,),
        in_specs=[
            pl.BlockSpec(depth.shape, lambda q: (0,) * 5),
            pl.BlockSpec((1, 2, span, columns), lambda q: (q, 0, 0, 0)),
        ]
        + [pl.BlockSpec(memory_space=pl.ANY)] * len(earlier),
        out_specs=pl.BlockSpec(
            (2, row_count, z1_part, width, columns), lambda q: (0, 0, 0, chunk, q)
        ),
        input_output_aliases={2: 0} if earlier else {},
        compiler_params=pltpu.CompilerParams(vmem_limit_bytes=VMEM_BYTES),
        cost_estimate=pl.CostEstimate(
            flops=8 * row_count * z1_part * width * span * pix_count * columns,
            bytes_accessed=28 * 1024 * 1024,
            transcendentals=0,
        ),
    )(depth, propagator, *earlier)


def on_device(raw_spectra, background, dispersion, propagator):
    _, row_count, wave_span, pix_local = raw_spectra.shape
    wave_count = lax.axis_size("wave")
    pix_count = lax.axis_size("pix")
    devices = wave_count * pix_count
    k0_count = 128
    k1_part = wave_span // k0_count
    k1_count = k1_part * wave_count
    width = k0_count // SEND_CHUNKS
    depth_width = k1_count // DEPTH_CHUNKS

    columns = lax.all_gather(propagator, "pix", axis=0, tiled=False)
    phases = jnp.stack((jnp.cos(dispersion), jnp.sin(dispersion), background))
    phases = phases.reshape(1, 3, k1_part, k0_count)
    phases = jnp.broadcast_to(phases, (wave_count,) + phases.shape[1:])
    phases = lax.all_to_all(phases, "wave", split_axis=0, concat_axis=0, tiled=True)
    phases = jnp.transpose(phases, (1, 3, 0, 2)).reshape(3, k0_count, k1_count)

    raw = raw_spectra.reshape(2, row_count, k1_part, k0_count, pix_local)
    highs, lows = [], []
    for chunk in range(SEND_CHUNKS):
        blocks = pack(raw, wave_count, chunk, width)
        blocks = lax.all_to_all(blocks, "wave", split_axis=0, concat_axis=0, tiled=True)
        high, low = coarse_stage(blocks, phases, chunk)
        highs.append(high)
        lows.append(low)
    image = None
    for chunk in range(DEPTH_CHUNKS):
        depth = fine_stage(highs, lows, devices, chunk, depth_width)
        depth = lax.all_to_all(depth, ("wave", "pix"), split_axis=0, concat_axis=0, tiled=True)
        image = refocus(depth, columns, row_count, chunk, DEPTH_CHUNKS, image)
    return image.reshape(2, row_count, -1, image.shape[4])


def solution(mesh):
    in_specs = (P(None, None, "wave", "pix"), P("wave"), P("wave"), P(None, None, "pix"))
    out_specs = P(None, None, ("wave", "pix"), None)
    return jax.shard_map(
        on_device, mesh=mesh, in_specs=in_specs, out_specs=out_specs, check_vma=False
    )
```

```python
import functools
import math

import jax
import jax.numpy as jnp
import numpy as np
from jax import lax
from jax.experimental import pallas as pl
from jax.experimental.pallas import tpu as pltpu
from jax.sharding import PartitionSpec as P

CHUNK = 16
VMEM_BYTES = 56 * 1024 * 1024


def unit_roots(rows, columns, modulus):
    product = np.outer(np.arange(rows), np.arange(columns)) % modulus
    angle = -2.0 * np.pi / modulus * product
    return np.cos(angle), np.sin(angle)


def split(value):
    high = value.astype(jnp.bfloat16)
    return high, (value - high.astype(jnp.float32)).astype(jnp.bfloat16)


def swap_halves(value):
    half = value.shape[-1] // 2
    if 2 * half == 128:
        return pltpu.roll(value, half, value.ndim - 1)
    return jnp.concatenate((value[..., half:], value[..., :half]), axis=-1)


def left_half(shape):
    return lax.broadcasted_iota(jnp.int32, shape, len(shape) - 1) < shape[-1] // 2


def pack_kernel(me_ref, raw_ref, *out_refs):
    count = len(out_refs)
    pixels = out_refs[0].shape[2] // 2
    for d in range(count):
        lanes = slice(d * pixels, (d + 1) * pixels)
        piece = jnp.concatenate((raw_ref[0, 0, :, :, lanes], raw_ref[1, 0, :, :, lanes]), axis=2)
        for m in range(count):

            @pl.when((me_ref[0] ^ m) == d)
            def _():
                out_refs[m][...] = piece


def pack(me, raw, wave_count, row):
    _, _, k1_part, k0_count, pix_local = raw.shape
    lanes = 2 * pix_local // wave_count
    span = min(4, k1_part)
    return pl.pallas_call(
        pack_kernel,
        out_shape=[jax.ShapeDtypeStruct((k1_part, k0_count, lanes), raw.dtype)] * wave_count,
        grid=(k1_part // span,),
        in_specs=[
            pl.BlockSpec(memory_space=pltpu.SMEM),
            pl.BlockSpec((2, 1, span, k0_count, pix_local), lambda k: (0, row, k, 0, 0)),
        ],
        out_specs=[pl.BlockSpec((span, k0_count, lanes), lambda k: (k, 0, 0))] * wave_count,
        compiler_params=pltpu.CompilerParams(vmem_limit_bytes=VMEM_BYTES),
        cost_estimate=pl.CostEstimate(
            flops=0, bytes_accessed=8 * k1_part * k0_count * pix_local, transcendentals=0
        ),
    )(me, raw)


def transform_kernel(steps, me_ref, *refs):
    x_refs = refs[:-9]
    phase_ref, small_ref, turn_ref, fine_ref, out_ref, data, high, low, part = refs[-9:]
    step = pl.program_id(0)
    k1_count, lanes = data.shape[1], data.shape[2]
    k1_part = x_refs[0].shape[0]
    sign = jnp.where(left_half((1, lanes)), -1.0, 1.0)

    @pl.when(step < steps)
    def _():
        for m, x_ref in enumerate(x_refs):
            start = pl.multiple_of((me_ref[0] ^ m) * k1_part, k1_part)
            block = jnp.swapaxes(x_ref[...].astype(jnp.float32), 0, 1)
            data[:, pl.ds(start, k1_part), :] = block.astype(jnp.bfloat16)
        for i in range(CHUNK):
            turn_real = turn_ref[0, 0, :, i : i + 1]
            turn_imag = turn_ref[1, 0, :, i : i + 1]
            cosine = phase_ref[0, i : i + 1, :]
            sine = phase_ref[1, i : i + 1, :]
            background = phase_ref[2, i : i + 1, :]
            small_real = small_ref[0] * turn_real - small_ref[1] * turn_imag
            small_imag = small_ref[0] * turn_imag + small_ref[1] * turn_real
            real = small_real * cosine - small_imag * sine
            imag = small_real * sine + small_imag * cosine
            base_real = jnp.sum(real * background, axis=1, keepdims=True)
            base_imag = jnp.sum(imag * background, axis=1, keepdims=True)
            real_high, real_low = split(real)
            imag_high, imag_low = split(imag)
            matrix = jnp.concatenate((real_high, imag_high, real_low, imag_low), axis=0)
            both = jnp.dot(matrix, data[i], preferred_element_type=jnp.float32)
            half = both.shape[0] // 2
            both = both[:half] + both[half:]
            by_real, by_imag = both[: half // 2], both[half // 2 :]
            base = jnp.where(left_half(by_real.shape), base_real, base_imag)
            part[i] = by_real + sign * swap_halves(by_imag) - base
        at = pl.ds(pl.multiple_of(step * CHUNK, CHUNK), CHUNK)
        turned_high, turned_low = split(jnp.swapaxes(part[...], 0, 1))
        high[:, at, :] = turned_high
        low[:, at, :] = turned_low

    @pl.when(step >= steps)
    def _():
        first = (step - steps) * CHUNK
        for i in range(0, CHUNK, 2):
            at = first + i
            columns = jnp.concatenate((high[at], high[at + 1]), axis=1)
            rest = jnp.concatenate((low[at], low[at + 1]), axis=1)
            both = jnp.dot(fine_ref[...], columns, preferred_element_type=jnp.float32)
            half = both.shape[0] // 2
            both = (
                both[:half]
                + both[half:]
                + jnp.dot(fine_ref[:half], rest, preferred_element_type=jnp.float32)
            )
            by_real, by_imag = both[: half // 2], both[half // 2 :]
            for j in range(2):
                own = slice(j * lanes, (j + 1) * lanes)
                part[i + j] = by_real[:, own] + sign * swap_halves(by_imag[:, own])
        turned = jnp.swapaxes(part[...], 0, 1).astype(jnp.bfloat16)
        out_ref[...] = turned.reshape(out_ref.shape)


def depth_transform(me, pieces, phases, devices):
    wave_count = len(pieces)
    k1_part, k0_count, lanes = pieces[0].shape
    k1_count = wave_count * k1_part
    length = k1_count * k0_count
    steps = k0_count // CHUNK
    small = np.stack(unit_roots(k1_count, k1_count, k1_count)).astype(np.float32)
    turn = np.stack(unit_roots(k1_count, k0_count, length)).astype(np.float32)
    turn = turn.reshape(2, k1_count, steps, CHUNK).transpose(0, 2, 1, 3)
    fine = np.concatenate(unit_roots(k0_count, k0_count, k0_count), axis=0) / math.sqrt(length)
    fine_high = fine.astype(jnp.bfloat16)
    fine_low = (fine - fine_high.astype(np.float64)).astype(jnp.bfloat16)
    fine = np.concatenate((fine_high, fine_low), axis=0)
    out_shape = (devices, k0_count // devices, k1_count, lanes)
    return pl.pallas_call(
        functools.partial(transform_kernel, steps),
        out_shape=jax.ShapeDtypeStruct(out_shape, jnp.bfloat16),
        grid=(2 * steps,),
        in_specs=[pl.BlockSpec(memory_space=pltpu.SMEM)]
        + [
            pl.BlockSpec((k1_part, CHUNK, lanes), lambda i: (0, jnp.minimum(i, steps - 1), 0))
        ]
        * wave_count
        + [
            pl.BlockSpec((3, CHUNK, k1_count), lambda i: (0, jnp.minimum(i, steps - 1), 0)),
            pl.BlockSpec(small.shape, lambda i: (0, 0, 0)),
            pl.BlockSpec(
                (2, 1, k1_count, CHUNK), lambda i: (0, jnp.minimum(i, steps - 1), 0, 0)
            ),
            pl.BlockSpec(fine.shape, lambda i: (0, 0)),
        ],
        out_specs=pl.BlockSpec(
            out_shape[:2] + (CHUNK, lanes), lambda i: (0, 0, jnp.maximum(i - steps, 0), 0)
        ),
        scratch_shapes=[
            pltpu.VMEM((CHUNK, k1_count, lanes), jnp.bfloat16),
            pltpu.VMEM((k1_count, k0_count, lanes), jnp.bfloat16),
            pltpu.VMEM((k1_count, k0_count, lanes), jnp.bfloat16),
            pltpu.VMEM((CHUNK, k1_count, lanes), jnp.float32),
        ],
        compiler_params=pltpu.CompilerParams(vmem_limit_bytes=VMEM_BYTES),
        cost_estimate=pl.CostEstimate(
            flops=20 * 128 * length * lanes, bytes_accessed=4 * length * lanes, transcendentals=0
        ),
    )(me, *pieces, phases, jnp.asarray(small), jnp.asarray(turn), jnp.asarray(fine))


def refocus_kernel(depth_ref, prop_ref, *rest):
    out_ref, rows = rest[-2:]
    senders, depths, lanes = depth_ref.shape

    @pl.when(pl.program_id(0) == 0)
    def _():
        sign = jnp.where(left_half((1, lanes)), 1.0, -1.0)
        for sender in range(senders):
            own = slice(sender * lanes, (sender + 1) * lanes)
            value = depth_ref[sender].astype(jnp.float32)
            rows[:depths, own] = (value * sign).astype(jnp.bfloat16)
            rows[depths:, own] = swap_halves(value).astype(jnp.bfloat16)

    columns = prop_ref[...].reshape(senders * lanes, prop_ref.shape[3])
    for c in range(2):
        out_ref[c, 0] = jnp.dot(
            rows[c * depths : (c + 1) * depths], columns, preferred_element_type=jnp.float32
        )


def refocus(depth, propagator, row, row_count, image):
    wave_count, pix_count, span, columns = propagator.shape
    senders, depths, lanes = depth.shape
    earlier = () if image is None else (image,)
    return pl.pallas_call(
        refocus_kernel,
        out_shape=jax.ShapeDtypeStruct(
            (2, row_count, depths, pix_count * columns), jnp.float32
        ),
        grid=(pix_count,),
        in_specs=[
            pl.BlockSpec(depth.shape, lambda q: (0, 0, 0)),
            pl.BlockSpec((wave_count, 1, span, columns), lambda q: (0, q, 0, 0)),
        ]
        + [pl.BlockSpec(memory_space=pl.ANY)] * len(earlier),
        out_specs=pl.BlockSpec((2, 1, depths, columns), lambda q: (0, row, 0, q)),
        input_output_aliases={2: 0} if earlier else {},
        scratch_shapes=[pltpu.VMEM((2 * depths, senders * lanes), jnp.bfloat16)],
        compiler_params=pltpu.CompilerParams(vmem_limit_bytes=VMEM_BYTES),
        cost_estimate=pl.CostEstimate(
            flops=4 * depths * senders * lanes * pix_count * columns,
            bytes_accessed=28 * 1024 * 1024,
            transcendentals=0,
        ),
    )(depth, propagator, *earlier)


def on_device(raw_spectra, background, dispersion, propagator):
    _, row_count, wave_span, pix_local = raw_spectra.shape
    wave_count = lax.axis_size("wave")
    pix_count = lax.axis_size("pix")
    devices = wave_count * pix_count
    pixels = pix_local // wave_count
    k0_count = 128
    k1_part = wave_span // k0_count
    k1_count = k1_part * wave_count
    wave_pos = lax.axis_index("wave")
    me = wave_pos.astype(jnp.int32).reshape(1)

    columns = propagator.reshape(2, pix_count, wave_count, pixels, pix_local)
    columns = lax.dynamic_index_in_dim(columns, wave_pos, axis=2, keepdims=False)
    columns = jnp.swapaxes(columns, 0, 1).reshape(2 * pix_count * pixels, pix_local)
    columns = lax.all_gather(columns, ("wave", "pix"), axis=0, tiled=False)
    columns = columns.reshape(wave_count, pix_count, -1, pix_local)

    phases = jnp.stack((jnp.cos(dispersion), jnp.sin(dispersion), background))
    phases = phases.reshape(1, 3, k1_part, k0_count)
    phases = jnp.broadcast_to(phases, (wave_count,) + phases.shape[1:])
    phases = lax.all_to_all(phases, "wave", split_axis=0, concat_axis=0, tiled=True)
    phases = jnp.transpose(phases, (1, 3, 0, 2)).reshape(3, k0_count, k1_count)

    raw = raw_spectra.reshape(2, row_count, k1_part, k0_count, pix_local)
    image = None
    arrived = ()
    for row in range(row_count):
        pieces = pack(me, raw, wave_count, row)
        if row > 0:
            pieces, arrived = lax.optimization_barrier((pieces, arrived))
        arrived = [pieces[0]] + [
            lax.ppermute(pieces[m], "wave", [(s, s ^ m) for s in range(wave_count)])
            for m in range(1, wave_count)
        ]
        depth = depth_transform(me, arrived, phases, devices)
        depth = depth.reshape(devices, -1, 2 * pixels)
        depth = lax.all_to_all(depth, ("wave", "pix"), split_axis=0, concat_axis=0, tiled=True)
        image = refocus(depth, columns, row, row_count, image)
    return image


def solution(mesh):
    in_specs = (P(None, None, "wave", "pix"), P("wave"), P("wave"), P(None, None, "pix"))
    out_specs = P(None, None, ("wave", "pix"), None)
    return jax.shard_map(
        on_device, mesh=mesh, in_specs=in_specs, out_specs=out_specs, check_vma=False
    )
```

```python
import functools
import math

import jax
import jax.numpy as jnp
import numpy as np
from jax import lax
from jax.experimental import pallas as pl
from jax.experimental.pallas import tpu as pltpu
from jax.sharding import PartitionSpec as P

CHUNK = 16
VMEM_BYTES = 56 * 1024 * 1024


def unit_roots(rows, columns, modulus):
    product = np.outer(np.arange(rows), np.arange(columns)) % modulus
    angle = -2.0 * np.pi / modulus * product
    return np.cos(angle), np.sin(angle)


def split(value):
    high = value.astype(jnp.bfloat16)
    return high, (value - high.astype(jnp.float32)).astype(jnp.bfloat16)


def swap_halves(value):
    half = value.shape[-1] // 2
    if 2 * half == 128:
        return pltpu.roll(value, half, value.ndim - 1)
    return jnp.concatenate((value[..., half:], value[..., :half]), axis=-1)


def left_half(shape):
    return lax.broadcasted_iota(jnp.int32, shape, len(shape) - 1) < shape[-1] // 2


def pack_kernel(me_ref, raw_ref, *out_refs):
    count = len(out_refs)
    pixels = out_refs[0].shape[2] // 2
    for me in range(count):

        @pl.when(me_ref[0] == me)
        def _():
            for m in range(count):
                lanes = slice((me ^ m) * pixels, (me ^ m) * pixels + pixels)
                parts = (raw_ref[0, 0, :, :, lanes], raw_ref[1, 0, :, :, lanes])
                out_refs[m][...] = jnp.concatenate(parts, axis=2)


def pack(me, raw, wave_count, row):
    _, _, k1_part, k0_count, pix_local = raw.shape
    lanes = 2 * pix_local // wave_count
    span = min(4, k1_part)
    return pl.pallas_call(
        pack_kernel,
        out_shape=[jax.ShapeDtypeStruct((k1_part, k0_count, lanes), raw.dtype)] * wave_count,
        grid=(k1_part // span,),
        in_specs=[
            pl.BlockSpec(memory_space=pltpu.SMEM),
            pl.BlockSpec((2, 1, span, k0_count, pix_local), lambda k: (0, row, k, 0, 0)),
        ],
        out_specs=[pl.BlockSpec((span, k0_count, lanes), lambda k: (k, 0, 0))] * wave_count,
        compiler_params=pltpu.CompilerParams(vmem_limit_bytes=VMEM_BYTES),
        cost_estimate=pl.CostEstimate(
            flops=0, bytes_accessed=8 * k1_part * k0_count * pix_local, transcendentals=0
        ),
    )(me, raw)


def matrix_kernel(phase_ref, small_ref, turn_ref, matrix_ref, base_ref):
    bases = []
    for i in range(CHUNK):
        turn_real = turn_ref[0, 0, :, i : i + 1]
        turn_imag = turn_ref[1, 0, :, i : i + 1]
        cosine = phase_ref[0, i : i + 1, :]
        sine = phase_ref[1, i : i + 1, :]
        background = phase_ref[2, i : i + 1, :]
        small_real = small_ref[0] * turn_real - small_ref[1] * turn_imag
        small_imag = small_ref[0] * turn_imag + small_ref[1] * turn_real
        real = small_real * cosine - small_imag * sine
        imag = small_real * sine + small_imag * cosine
        bases.append([jnp.sum(v * background, axis=1, keepdims=True) for v in (real, imag)])
        real_high, real_low = split(real)
        imag_high, imag_low = split(imag)
        count = real.shape[0]
        matrix_ref[i, :count] = jnp.concatenate((real_high, imag_high), axis=1)
        matrix_ref[i, count:] = jnp.concatenate((real_low, imag_low), axis=1)
    for c in range(2):
        base_ref[c, 0] = jnp.concatenate([base[c] for base in bases], axis=1)


def stage_matrices(phases):
    _, k0_count, k1_count = phases.shape
    length = k1_count * k0_count
    steps = k0_count // CHUNK
    small = np.stack(unit_roots(k1_count, k1_count, k1_count)).astype(np.float32)
    turn = np.stack(unit_roots(k1_count, k0_count, length)).astype(np.float32)
    turn = turn.reshape(2, k1_count, steps, CHUNK).transpose(0, 2, 1, 3)
    column_spec = pl.BlockSpec((2, 1, k1_count, CHUNK), lambda i: (0, i, 0, 0))
    return pl.pallas_call(
        matrix_kernel,
        out_shape=(
            jax.ShapeDtypeStruct((k0_count, 2 * k1_count, 2 * k1_count), jnp.bfloat16),
            jax.ShapeDtypeStruct((2, steps, k1_count, CHUNK), jnp.float32),
        ),
        grid=(steps,),
        in_specs=[
            pl.BlockSpec((3, CHUNK, k1_count), lambda i: (0, i, 0)),
            pl.BlockSpec(small.shape, lambda i: (0, 0, 0)),
            column_spec,
        ],
        out_specs=(
            pl.BlockSpec((CHUNK, 2 * k1_count, 2 * k1_count), lambda i: (i, 0, 0)),
            column_spec,
        ),
        compiler_params=pltpu.CompilerParams(vmem_limit_bytes=VMEM_BYTES),
        cost_estimate=pl.CostEstimate(
            flops=20 * length * k1_count, bytes_accessed=8 * length * k1_count, transcendentals=0
        ),
    )(phases, jnp.asarray(small), jnp.asarray(turn))


def transform_kernel(steps, me_ref, *refs):
    x_refs = refs[:-7]
    matrix_ref, base_ref, fine_ref, out_ref, data, middle, part = refs[-7:]
    step = pl.program_id(0)
    k1_count, lanes = data.shape[1] // 2, data.shape[2]
    k0_count = middle.shape[1] // 2
    k1_part = x_refs[0].shape[0]
    sign = jnp.where(left_half((1, lanes)), -1.0, 1.0)

    @pl.when(step < steps)
    def _():
        for m, x_ref in enumerate(x_refs):
            start = pl.multiple_of((me_ref[0] ^ m) * k1_part, k1_part)
            block = jnp.swapaxes(x_ref[...].astype(jnp.float32), 0, 1)
            data[:, pl.ds(start, k1_part), :] = block.astype(jnp.bfloat16)
            other = swap_halves(block) * sign
            data[:, pl.ds(k1_count + start, k1_part), :] = other.astype(jnp.bfloat16)
        for i in range(CHUNK):
            both = jnp.dot(matrix_ref[i], data[i], preferred_element_type=jnp.float32)
            base = jnp.where(
                left_half((k1_count, lanes)),
                base_ref[0, 0, :, i : i + 1],
                base_ref[1, 0, :, i : i + 1],
            )
            part[i] = both[:k1_count] + both[k1_count:] - base
        at = pl.multiple_of(step * CHUNK, CHUNK)
        turned_high, turned_low = split(jnp.swapaxes(part[...], 0, 1))
        middle[:, pl.ds(at, CHUNK), :] = turned_high
        middle[:, pl.ds(k0_count + at, CHUNK), :] = turned_low

    @pl.when(step >= steps)
    def _():
        first = (step - steps) * CHUNK
        for i in range(0, CHUNK, 2):
            at = first + i
            columns = jnp.concatenate((middle[at], middle[at + 1]), axis=1)
            both = jnp.dot(fine_ref[...], columns, preferred_element_type=jnp.float32)
            half = both.shape[0] // 2
            both = both[:half] + both[half:]
            by_real, by_imag = both[: half // 2], both[half // 2 :]
            for j in range(2):
                own = slice(j * lanes, (j + 1) * lanes)
                part[i + j] = by_real[:, own] + sign * swap_halves(by_imag[:, own])
        turned = jnp.swapaxes(part[...], 0, 1).astype(jnp.bfloat16)
        out_ref[...] = turned.reshape(out_ref.shape)


def depth_transform(me, pieces, matrices, base, devices):
    wave_count = len(pieces)
    k1_part, k0_count, lanes = pieces[0].shape
    k1_count = wave_count * k1_part
    length = k1_count * k0_count
    steps = k0_count // CHUNK
    fine = np.concatenate(unit_roots(k0_count, k0_count, k0_count), axis=0) / math.sqrt(length)
    fine_high = fine.astype(jnp.bfloat16)
    fine_low = (fine - fine_high.astype(np.float64)).astype(jnp.bfloat16)
    fine = np.concatenate((fine_high, fine_low), axis=0)
    fine = np.concatenate((fine, fine), axis=1)
    out_shape = (devices, k0_count // devices, k1_count, lanes)
    return pl.pallas_call(
        functools.partial(transform_kernel, steps),
        out_shape=jax.ShapeDtypeStruct(out_shape, jnp.bfloat16),
        grid=(2 * steps,),
        in_specs=[pl.BlockSpec(memory_space=pltpu.SMEM)]
        + [
            pl.BlockSpec((k1_part, CHUNK, lanes), lambda i: (0, jnp.minimum(i, steps - 1), 0))
        ]
        * wave_count
        + [
            pl.BlockSpec(
                (CHUNK, 2 * k1_count, 2 * k1_count), lambda i: (jnp.minimum(i, steps - 1), 0, 0)
            ),
            pl.BlockSpec(
                (2, 1, k1_count, CHUNK), lambda i: (0, jnp.minimum(i, steps - 1), 0, 0)
            ),
            pl.BlockSpec(fine.shape, lambda i: (0, 0)),
        ],
        out_specs=pl.BlockSpec(
            out_shape[:2] + (CHUNK, lanes), lambda i: (0, 0, jnp.maximum(i - steps, 0), 0)
        ),
        scratch_shapes=[
            pltpu.VMEM((CHUNK, 2 * k1_count, lanes), jnp.bfloat16),
            pltpu.VMEM((k1_count, 2 * k0_count, lanes), jnp.bfloat16),
            pltpu.VMEM((CHUNK, k1_count, lanes), jnp.float32),
        ],
        compiler_params=pltpu.CompilerParams(vmem_limit_bytes=VMEM_BYTES),
        cost_estimate=pl.CostEstimate(
            flops=20 * 128 * length * lanes, bytes_accessed=12 * length * lanes, transcendentals=0
        ),
    )(me, *pieces, matrices, base, jnp.asarray(fine))


def refocus_kernel(depth_ref, prop_ref, *rest):
    out_ref, rows = rest[-2:]
    senders, depths, lanes = depth_ref.shape

    @pl.when(pl.program_id(0) == 0)
    def _():
        sign = jnp.where(left_half((1, lanes)), 1.0, -1.0)
        for sender in range(senders):
            own = slice(sender * lanes, (sender + 1) * lanes)
            value = depth_ref[sender].astype(jnp.float32)
            rows[:depths, own] = (value * sign).astype(jnp.bfloat16)
            rows[depths:, own] = swap_halves(value).astype(jnp.bfloat16)

    columns = prop_ref[...].reshape(senders * lanes, prop_ref.shape[3])
    for c in range(2):
        out_ref[c, 0] = jnp.dot(
            rows[c * depths : (c + 1) * depths], columns, preferred_element_type=jnp.float32
        )


def refocus(depth, propagator, row, row_count, image):
    wave_count, pix_count, span, columns = propagator.shape
    senders, depths, lanes = depth.shape
    earlier = () if image is None else (image,)
    return pl.pallas_call(
        refocus_kernel,
        out_shape=jax.ShapeDtypeStruct(
            (2, row_count, depths, pix_count * columns), jnp.float32
        ),
        grid=(pix_count,),
        in_specs=[
            pl.BlockSpec(depth.shape, lambda q: (0, 0, 0)),
            pl.BlockSpec((wave_count, 1, span, columns), lambda q: (0, q, 0, 0)),
        ]
        + [pl.BlockSpec(memory_space=pl.ANY)] * len(earlier),
        out_specs=pl.BlockSpec((2, 1, depths, columns), lambda q: (0, row, 0, q)),
        input_output_aliases={2: 0} if earlier else {},
        scratch_shapes=[pltpu.VMEM((2 * depths, senders * lanes), jnp.bfloat16)],
        compiler_params=pltpu.CompilerParams(vmem_limit_bytes=VMEM_BYTES),
        cost_estimate=pl.CostEstimate(
            flops=4 * depths * senders * lanes * pix_count * columns,
            bytes_accessed=28 * 1024 * 1024,
            transcendentals=0,
        ),
    )(depth, propagator, *earlier)


def on_device(raw_spectra, background, dispersion, propagator):
    _, row_count, wave_span, pix_local = raw_spectra.shape
    wave_count = lax.axis_size("wave")
    pix_count = lax.axis_size("pix")
    devices = wave_count * pix_count
    pixels = pix_local // wave_count
    k0_count = 128
    k1_part = wave_span // k0_count
    k1_count = k1_part * wave_count
    wave_pos = lax.axis_index("wave")
    me = wave_pos.astype(jnp.int32).reshape(1)

    columns = propagator.reshape(2, pix_count, wave_count, pixels, pix_local)
    columns = lax.dynamic_index_in_dim(columns, wave_pos, axis=2, keepdims=False)
    columns = jnp.swapaxes(columns, 0, 1).reshape(2 * pix_count * pixels, pix_local)
    columns = lax.all_gather(columns, "pix", axis=0, tiled=False)
    columns = lax.all_gather(columns, "wave", axis=0, tiled=False)

    phases = jnp.stack((jnp.cos(dispersion), jnp.sin(dispersion), background))
    phases = phases.reshape(1, 3, k1_part, k0_count)
    phases = jnp.broadcast_to(phases, (wave_count,) + phases.shape[1:])
    phases = lax.all_to_all(phases, "wave", split_axis=0, concat_axis=0, tiled=True)
    phases = jnp.transpose(phases, (1, 3, 0, 2)).reshape(3, k0_count, k1_count)

    raw = raw_spectra.reshape(2, row_count, k1_part, k0_count, pix_local)
    packed = [pack(me, raw, wave_count, row) for row in range(row_count)]
    packed[0], phases = lax.optimization_barrier((packed[0], phases))
    matrices, base = stage_matrices(phases)
    image = None
    for row in range(row_count):
        arrived = [packed[row][0]] + [
            lax.ppermute(packed[row][m], "wave", [(s, s ^ m) for s in range(wave_count)])
            for m in range(1, wave_count)
        ]
        if row + 1 < row_count:
            arrived, packed[row + 1] = lax.optimization_barrier((arrived, packed[row + 1]))
        depth = depth_transform(me, arrived, matrices, base, devices)
        depth = depth.reshape(devices, -1, 2 * pixels)
        depth = lax.all_to_all(depth, ("wave", "pix"), split_axis=0, concat_axis=0, tiled=True)
        image = refocus(depth, columns, row, row_count, image)
    return image


def solution(mesh):
    in_specs = (P(None, None, "wave", "pix"), P("wave"), P("wave"), P(None, None, "pix"))
    out_specs = P(None, None, ("wave", "pix"), None)
    return jax.shard_map(
        on_device, mesh=mesh, in_specs=in_specs, out_specs=out_specs, check_vma=False
    )
```

```python
import functools
import math

import jax
import jax.numpy as jnp
import numpy as np
from jax import lax
from jax.experimental import pallas as pl
from jax.experimental.pallas import tpu as pltpu
from jax.sharding import PartitionSpec as P

CHUNK = 16
VMEM_BYTES = 56 * 1024 * 1024


def unit_roots(rows, columns, modulus):
    product = np.outer(np.arange(rows), np.arange(columns)) % modulus
    angle = -2.0 * np.pi / modulus * product
    return np.cos(angle), np.sin(angle)


def split(value):
    high = value.astype(jnp.bfloat16)
    return high, (value - high.astype(jnp.float32)).astype(jnp.bfloat16)


def swap_halves(value):
    half = value.shape[-1] // 2
    if 2 * half == 128:
        return pltpu.roll(value, half, value.ndim - 1)
    return jnp.concatenate((value[..., half:], value[..., :half]), axis=-1)


def left_half(shape):
    return lax.broadcasted_iota(jnp.int32, shape, len(shape) - 1) < shape[-1] // 2


def pack_kernel(me_ref, raw_ref, *out_refs):
    count = len(out_refs)
    pixels = out_refs[0].shape[2] // 2
    for me in range(count):

        @pl.when(me_ref[0] == me)
        def _():
            for m in range(count):
                lanes = slice((me ^ m) * pixels, (me ^ m) * pixels + pixels)
                parts = (raw_ref[0, 0, :, :, lanes], raw_ref[1, 0, :, :, lanes])
                out_refs[m][...] = jnp.concatenate(parts, axis=2)


def pack(me, raw, wave_count, row):
    _, _, k1_part, k0_count, pix_local = raw.shape
    lanes = 2 * pix_local // wave_count
    span = min(4, k1_part)
    return pl.pallas_call(
        pack_kernel,
        out_shape=[jax.ShapeDtypeStruct((k1_part, k0_count, lanes), raw.dtype)] * wave_count,
        grid=(k1_part // span,),
        in_specs=[
            pl.BlockSpec(memory_space=pltpu.SMEM),
            pl.BlockSpec((2, 1, span, k0_count, pix_local), lambda k: (0, row, k, 0, 0)),
        ],
        out_specs=[pl.BlockSpec((span, k0_count, lanes), lambda k: (k, 0, 0))] * wave_count,
        compiler_params=pltpu.CompilerParams(vmem_limit_bytes=VMEM_BYTES),
        cost_estimate=pl.CostEstimate(
            flops=0, bytes_accessed=8 * k1_part * k0_count * pix_local, transcendentals=0
        ),
    )(me, raw)


def matrix_kernel(phase_ref, small_ref, turn_ref, matrix_ref, base_ref):
    bases = []
    for i in range(CHUNK):
        turn_real = turn_ref[0, 0, :, i : i + 1]
        turn_imag = turn_ref[1, 0, :, i : i + 1]
        cosine = phase_ref[0, i : i + 1, :]
        sine = phase_ref[1, i : i + 1, :]
        background = phase_ref[2, i : i + 1, :]
        small_real = small_ref[0] * turn_real - small_ref[1] * turn_imag
        small_imag = small_ref[0] * turn_imag + small_ref[1] * turn_real
        real = small_real * cosine - small_imag * sine
        imag = small_real * sine + small_imag * cosine
        bases.append([jnp.sum(v * background, axis=1, keepdims=True) for v in (real, imag)])
        real_high, real_low = split(real)
        imag_high, imag_low = split(imag)
        count = real.shape[0]
        matrix_ref[i, :count] = jnp.concatenate((real_high, imag_high), axis=1)
        matrix_ref[i, count:] = jnp.concatenate((real_low, imag_low), axis=1)
    for c in range(2):
        base_ref[c, 0] = jnp.concatenate([base[c] for base in bases], axis=1)


def stage_matrices(phases):
    _, k0_count, k1_count = phases.shape
    length = k1_count * k0_count
    steps = k0_count // CHUNK
    small = np.stack(unit_roots(k1_count, k1_count, k1_count)).astype(np.float32)
    turn = np.stack(unit_roots(k1_count, k0_count, length)).astype(np.float32)
    turn = turn.reshape(2, k1_count, steps, CHUNK).transpose(0, 2, 1, 3)
    column_spec = pl.BlockSpec((2, 1, k1_count, CHUNK), lambda i: (0, i, 0, 0))
    return pl.pallas_call(
        matrix_kernel,
        out_shape=(
            jax.ShapeDtypeStruct((k0_count, 2 * k1_count, 2 * k1_count), jnp.bfloat16),
            jax.ShapeDtypeStruct((2, steps, k1_count, CHUNK), jnp.float32),
        ),
        grid=(steps,),
        in_specs=[
            pl.BlockSpec((3, CHUNK, k1_count), lambda i: (0, i, 0)),
            pl.BlockSpec(small.shape, lambda i: (0, 0, 0)),
            column_spec,
        ],
        out_specs=(
            pl.BlockSpec((CHUNK, 2 * k1_count, 2 * k1_count), lambda i: (i, 0, 0)),
            column_spec,
        ),
        compiler_params=pltpu.CompilerParams(vmem_limit_bytes=VMEM_BYTES),
        cost_estimate=pl.CostEstimate(
            flops=20 * length * k1_count, bytes_accessed=8 * length * k1_count, transcendentals=0
        ),
    )(phases, jnp.asarray(small), jnp.asarray(turn))


def transform_kernel(steps, me_ref, *refs):
    x_refs = refs[:-7]
    matrix_ref, base_ref, fine_ref, out_ref, data, middle, part = refs[-7:]
    step = pl.program_id(0)
    k1_count, lanes = data.shape[1] // 2, data.shape[2]
    k0_count = middle.shape[1] // 2
    k1_part = x_refs[0].shape[0]
    sign = jnp.where(left_half((1, lanes)), -1.0, 1.0)

    @pl.when(step < steps)
    def _():
        for m, x_ref in enumerate(x_refs):
            start = pl.multiple_of((me_ref[0] ^ m) * k1_part, k1_part)
            block = jnp.swapaxes(x_ref[...].astype(jnp.float32), 0, 1)
            data[:, pl.ds(start, k1_part), :] = block.astype(jnp.bfloat16)
            other = swap_halves(block) * sign
            data[:, pl.ds(k1_count + start, k1_part), :] = other.astype(jnp.bfloat16)
        for i in range(CHUNK):
            both = jnp.dot(matrix_ref[i], data[i], preferred_element_type=jnp.float32)
            base = jnp.where(
                left_half((k1_count, lanes)),
                base_ref[0, 0, :, i : i + 1],
                base_ref[1, 0, :, i : i + 1],
            )
            part[i] = both[:k1_count] + both[k1_count:] - base
        at = pl.multiple_of(step * CHUNK, CHUNK)
        turned_high, turned_low = split(jnp.swapaxes(part[...], 0, 1))
        middle[:, pl.ds(at, CHUNK), :] = turned_high
        middle[:, pl.ds(k0_count + at, CHUNK), :] = turned_low

    @pl.when(step >= steps)
    def _():
        first = (step - steps) * CHUNK
        for i in range(0, CHUNK, 2):
            at = first + i
            columns = jnp.concatenate((middle[at], middle[at + 1]), axis=1)
            both = jnp.dot(fine_ref[...], columns, preferred_element_type=jnp.float32)
            half = both.shape[0] // 2
            both = both[:half] + both[half:]
            by_real, by_imag = both[: half // 2], both[half // 2 :]
            for j in range(2):
                own = slice(j * lanes, (j + 1) * lanes)
                part[i + j] = by_real[:, own] + sign * swap_halves(by_imag[:, own])
        turned = jnp.swapaxes(part[...], 0, 1).astype(jnp.bfloat16)
        out_ref[...] = turned.reshape(out_ref.shape)


def depth_transform(me, pieces, matrices, base, devices):
    wave_count = len(pieces)
    k1_part, k0_count, lanes = pieces[0].shape
    k1_count = wave_count * k1_part
    length = k1_count * k0_count
    steps = k0_count // CHUNK
    fine = np.concatenate(unit_roots(k0_count, k0_count, k0_count), axis=0) / math.sqrt(length)
    fine_high = fine.astype(jnp.bfloat16)
    fine_low = (fine - fine_high.astype(np.float64)).astype(jnp.bfloat16)
    fine = np.concatenate((fine_high, fine_low), axis=0)
    fine = np.concatenate((fine, fine), axis=1)
    out_shape = (devices, k0_count // devices, k1_count, lanes)
    return pl.pallas_call(
        functools.partial(transform_kernel, steps),
        out_shape=jax.ShapeDtypeStruct(out_shape, jnp.bfloat16),
        grid=(2 * steps,),
        in_specs=[pl.BlockSpec(memory_space=pltpu.SMEM)]
        + [
            pl.BlockSpec((k1_part, CHUNK, lanes), lambda i: (0, jnp.minimum(i, steps - 1), 0))
        ]
        * wave_count
        + [
            pl.BlockSpec(
                (CHUNK, 2 * k1_count, 2 * k1_count), lambda i: (jnp.minimum(i, steps - 1), 0, 0)
            ),
            pl.BlockSpec(
                (2, 1, k1_count, CHUNK), lambda i: (0, jnp.minimum(i, steps - 1), 0, 0)
            ),
            pl.BlockSpec(fine.shape, lambda i: (0, 0)),
        ],
        out_specs=pl.BlockSpec(
            out_shape[:2] + (CHUNK, lanes), lambda i: (0, 0, jnp.maximum(i - steps, 0), 0)
        ),
        scratch_shapes=[
            pltpu.VMEM((CHUNK, 2 * k1_count, lanes), jnp.bfloat16),
            pltpu.VMEM((k1_count, 2 * k0_count, lanes), jnp.bfloat16),
            pltpu.VMEM((CHUNK, k1_count, lanes), jnp.float32),
        ],
        compiler_params=pltpu.CompilerParams(vmem_limit_bytes=VMEM_BYTES),
        cost_estimate=pl.CostEstimate(
            flops=20 * 128 * length * lanes, bytes_accessed=12 * length * lanes, transcendentals=0
        ),
    )(me, *pieces, matrices, base, jnp.asarray(fine))


def even_mask(mask):
    return bin(mask).count("1") % 2 == 0


def refocus_kernel(wave_count, pix_count, me_ref, depth_ref, *refs):
    prop_refs = refs[: 2 * wave_count]
    out_ref, rows = refs[-2:]
    _, depths, lanes = depth_ref.shape
    half = pix_count // 2
    core = me_ref[1]

    @pl.when(pl.program_id(0) == 0)
    def _():
        sign = jnp.where(left_half((1, lanes)), 1.0, -1.0)
        for m in range(wave_count):
            first = (me_ref[0] ^ m) * pix_count
            for h in range(2):
                start = first + (h if even_mask(m) else core ^ h) * half
                for p in range(half):
                    at = (m * pix_count + h * half + p) * lanes
                    own = slice(at, at + lanes)
                    value = depth_ref[start + p].astype(jnp.float32)
                    rows[:depths, own] = (value * sign).astype(jnp.bfloat16)
                    rows[depths:, own] = swap_halves(value).astype(jnp.bfloat16)

    columns = jnp.concatenate([ref[0] for ref in prop_refs], axis=0)
    for c in range(2):
        out_ref[c, 0] = jnp.dot(
            rows[c * depths : (c + 1) * depths], columns, preferred_element_type=jnp.float32
        )


def refocus(me, depth, slices, row, row_count, image):
    wave_count = len(slices)
    senders, depths, lanes = depth.shape
    pix_count = senders // wave_count
    span = pix_count // 2 * lanes
    columns = slices[0][0].shape[2]
    operands, specs = [], []
    for mask in range(wave_count):
        for h in range(2):
            if even_mask(mask):
                operands.append(slices[mask][0])
                specs.append(pl.BlockSpec((1, span, columns), lambda q, h=h: (q, h, 0)))
            else:
                operands.append(slices[mask][h])
                specs.append(pl.BlockSpec((1, span, columns), lambda q: (q, 0, 0)))
    earlier = () if image is None else (image,)
    return pl.pallas_call(
        functools.partial(refocus_kernel, wave_count, pix_count),
        out_shape=jax.ShapeDtypeStruct(
            (2, row_count, depths, pix_count * columns), jnp.float32
        ),
        grid=(pix_count,),
        in_specs=[
            pl.BlockSpec(memory_space=pltpu.SMEM),
            pl.BlockSpec(depth.shape, lambda q: (0, 0, 0)),
        ]
        + specs
        + [pl.BlockSpec(memory_space=pl.ANY)] * len(earlier),
        out_specs=pl.BlockSpec((2, 1, depths, columns), lambda q: (0, row, 0, q)),
        input_output_aliases={2 + len(operands): 0} if earlier else {},
        scratch_shapes=[pltpu.VMEM((2 * depths, senders * lanes), jnp.bfloat16)],
        compiler_params=pltpu.CompilerParams(vmem_limit_bytes=VMEM_BYTES),
        cost_estimate=pl.CostEstimate(
            flops=4 * depths * senders * lanes * pix_count * columns,
            bytes_accessed=28 * 1024 * 1024,
            transcendentals=0,
        ),
    )(me, depth, *operands, *earlier)


def gather_slices(propagator, wave_pos, wave_count):
    _, span, pix_local = propagator.shape
    pix_count = lax.axis_size("pix")
    rows = propagator.reshape(2, pix_count, wave_count, -1, pix_local)
    slices = {}
    for mask in range(wave_count):
        if even_mask(mask):
            own = lax.dynamic_index_in_dim(rows, wave_pos ^ mask, axis=2, keepdims=False)
            own = jnp.swapaxes(own, 0, 1).reshape(2 * span // wave_count, pix_local)
            slices[mask] = [lax.all_gather(own, "pix", axis=0, tiled=False)]
    return slices


def exchange_slices(slices, wave_count, core):
    pix_count = lax.axis_size("pix")
    result = dict(slices)
    for mask in range(wave_count):
        if not even_mask(mask):
            bit = mask & -mask
            source = slices[mask ^ bit][0]
            half = source.shape[1] // 2
            own = lax.dynamic_slice_in_dim(source, core * half, half, axis=1)
            own = lax.ppermute(own, "wave", [(s, s ^ bit) for s in range(wave_count)])
            mate = lax.ppermute(own, "pix", [(s, s ^ 1) for s in range(pix_count)])
            result[mask] = [own, mate]
    return result


def on_device(raw_spectra, background, dispersion, propagator):
    _, row_count, wave_span, pix_local = raw_spectra.shape
    wave_count = lax.axis_size("wave")
    pix_count = lax.axis_size("pix")
    devices = wave_count * pix_count
    pixels = pix_local // wave_count
    k0_count = 128
    k1_part = wave_span // k0_count
    k1_count = k1_part * wave_count
    wave_pos = lax.axis_index("wave")
    core = lax.axis_index("pix") % 2
    me = jnp.stack((wave_pos, core)).astype(jnp.int32)
    slices = gather_slices(propagator, wave_pos, wave_count)

    phases = jnp.stack((jnp.cos(dispersion), jnp.sin(dispersion), background))
    phases = phases.reshape(1, 3, k1_part, k0_count)
    phases = jnp.broadcast_to(phases, (wave_count,) + phases.shape[1:])
    phases = lax.all_to_all(phases, "wave", split_axis=0, concat_axis=0, tiled=True)
    phases = jnp.transpose(phases, (1, 3, 0, 2)).reshape(3, k0_count, k1_count)

    raw = raw_spectra.reshape(2, row_count, k1_part, k0_count, pix_local)
    packed = [pack(me, raw, wave_count, row) for row in range(row_count)]
    packed[0], phases = lax.optimization_barrier((packed[0], phases))
    matrices, base = stage_matrices(phases)
    image = None
    for row in range(row_count):
        arrived = [packed[row][0]] + [
            lax.ppermute(packed[row][m], "wave", [(s, s ^ m) for s in range(wave_count)])
            for m in range(1, wave_count)
        ]
        if row + 1 < row_count:
            arrived, packed[row + 1] = lax.optimization_barrier((arrived, packed[row + 1]))
        if row == 0:
            slices[0], _ = lax.optimization_barrier((slices[0], arrived[1]))
            slices = exchange_slices(slices, wave_count, core)
        depth = depth_transform(me, arrived, matrices, base, devices)
        depth = depth.reshape(devices, -1, 2 * pixels)
        depth = lax.all_to_all(depth, ("wave", "pix"), split_axis=0, concat_axis=0, tiled=True)
        image = refocus(me, depth, slices, row, row_count, image)
    return image


def solution(mesh):
    in_specs = (P(None, None, "wave", "pix"), P("wave"), P("wave"), P(None, None, "pix"))
    out_specs = P(None, None, ("wave", "pix"), None)
    return jax.shard_map(
        on_device, mesh=mesh, in_specs=in_specs, out_specs=out_specs, check_vma=False
    )
```

```python
import functools
import math

import jax
import jax.numpy as jnp
import numpy as np
from jax import lax
from jax.experimental import pallas as pl
from jax.experimental.pallas import tpu as pltpu
from jax.sharding import PartitionSpec as P

CHUNK = 16
MATRIX_COST = 120 * 10**9
VMEM_BYTES = 56 * 1024 * 1024


def unit_roots(rows, columns, modulus):
    product = np.outer(np.arange(rows), np.arange(columns)) % modulus
    angle = -2.0 * np.pi / modulus * product
    return np.cos(angle), np.sin(angle)


def split(value):
    high = value.astype(jnp.bfloat16)
    return high, (value - high.astype(jnp.float32)).astype(jnp.bfloat16)


def swap_halves(value):
    half = value.shape[-1] // 2
    if 2 * half == 128:
        return pltpu.roll(value, half, value.ndim - 1)
    return jnp.concatenate((value[..., half:], value[..., :half]), axis=-1)


def left_half(shape):
    return lax.broadcasted_iota(jnp.int32, shape, len(shape) - 1) < shape[-1] // 2


def pack_kernel(me_ref, raw_ref, *out_refs):
    count = len(out_refs)
    pixels = out_refs[0].shape[2] // 2
    for me in range(count):

        @pl.when(me_ref[0] == me)
        def _():
            for m in range(count):
                lanes = slice((me ^ m) * pixels, (me ^ m) * pixels + pixels)
                parts = (raw_ref[0, 0, :, :, lanes], raw_ref[1, 0, :, :, lanes])
                out_refs[m][...] = jnp.concatenate(parts, axis=2)


def pack(me, raw, wave_count, row):
    _, _, k1_part, k0_count, pix_local = raw.shape
    lanes = 2 * pix_local // wave_count
    span = min(4, k1_part)
    return pl.pallas_call(
        pack_kernel,
        out_shape=[jax.ShapeDtypeStruct((k1_part, k0_count, lanes), raw.dtype)] * wave_count,
        grid=(k1_part // span,),
        in_specs=[
            pl.BlockSpec(memory_space=pltpu.SMEM),
            pl.BlockSpec((2, 1, span, k0_count, pix_local), lambda k: (0, row, k, 0, 0)),
        ],
        out_specs=[pl.BlockSpec((span, k0_count, lanes), lambda k: (k, 0, 0))] * wave_count,
        compiler_params=pltpu.CompilerParams(vmem_limit_bytes=VMEM_BYTES),
        cost_estimate=pl.CostEstimate(
            flops=0, bytes_accessed=8 * k1_part * k0_count * pix_local, transcendentals=0
        ),
    )(me, raw)


def matrix_kernel(phase_ref, small_ref, turn_ref, matrix_ref, base_ref):
    bases = []
    for i in range(CHUNK):
        turn_real = turn_ref[0, 0, :, i : i + 1]
        turn_imag = turn_ref[1, 0, :, i : i + 1]
        cosine = phase_ref[0, i : i + 1, :]
        sine = phase_ref[1, i : i + 1, :]
        background = phase_ref[2, i : i + 1, :]
        small_real = small_ref[0] * turn_real - small_ref[1] * turn_imag
        small_imag = small_ref[0] * turn_imag + small_ref[1] * turn_real
        real = small_real * cosine - small_imag * sine
        imag = small_real * sine + small_imag * cosine
        bases.append([jnp.sum(v * background, axis=1, keepdims=True) for v in (real, imag)])
        real_high, real_low = split(real)
        imag_high, imag_low = split(imag)
        count = real.shape[0]
        matrix_ref[i, :count] = jnp.concatenate((real_high, imag_high), axis=1)
        matrix_ref[i, count:] = jnp.concatenate((real_low, imag_low), axis=1)
    for c in range(2):
        base_ref[c, 0] = jnp.concatenate([base[c] for base in bases], axis=1)


def stage_matrices(phases):
    _, k0_count, k1_count = phases.shape
    length = k1_count * k0_count
    steps = k0_count // CHUNK
    small = np.stack(unit_roots(k1_count, k1_count, k1_count)).astype(np.float32)
    turn = np.stack(unit_roots(k1_count, k0_count, length)).astype(np.float32)
    turn = turn.reshape(2, k1_count, steps, CHUNK).transpose(0, 2, 1, 3)
    column_spec = pl.BlockSpec((2, 1, k1_count, CHUNK), lambda i: (0, i, 0, 0))
    return pl.pallas_call(
        matrix_kernel,
        out_shape=(
            jax.ShapeDtypeStruct((k0_count, 2 * k1_count, 2 * k1_count), jnp.bfloat16),
            jax.ShapeDtypeStruct((2, steps, k1_count, CHUNK), jnp.float32),
        ),
        grid=(steps,),
        in_specs=[
            pl.BlockSpec((3, CHUNK, k1_count), lambda i: (0, i, 0)),
            pl.BlockSpec(small.shape, lambda i: (0, 0, 0)),
            column_spec,
        ],
        out_specs=(
            pl.BlockSpec((CHUNK, 2 * k1_count, 2 * k1_count), lambda i: (i, 0, 0)),
            column_spec,
        ),
        compiler_params=pltpu.CompilerParams(vmem_limit_bytes=VMEM_BYTES),
        cost_estimate=pl.CostEstimate(
            flops=20 * length * k1_count, bytes_accessed=8 * length * k1_count, transcendentals=0
        ),
    )(phases, jnp.asarray(small), jnp.asarray(turn))


def transform_kernel(steps, me_ref, *refs):
    x_refs = refs[:-7]
    matrix_ref, base_ref, fine_ref, out_ref, data, middle, part = refs[-7:]
    step = pl.program_id(0)
    k1_count, lanes = data.shape[1] // 2, data.shape[2]
    k0_count = middle.shape[1] // 2
    k1_part = x_refs[0].shape[0]
    sign = jnp.where(left_half((1, lanes)), -1.0, 1.0)

    @pl.when(step < steps)
    def _():
        for m, x_ref in enumerate(x_refs):
            start = pl.multiple_of((me_ref[0] ^ m) * k1_part, k1_part)
            block = jnp.swapaxes(x_ref[...].astype(jnp.float32), 0, 1)
            data[:, pl.ds(start, k1_part), :] = block.astype(jnp.bfloat16)
            other = swap_halves(block) * sign
            data[:, pl.ds(k1_count + start, k1_part), :] = other.astype(jnp.bfloat16)
        for i in range(CHUNK):
            both = jnp.dot(matrix_ref[i], data[i], preferred_element_type=jnp.float32)
            base = jnp.where(
                left_half((k1_count, lanes)),
                base_ref[0, 0, :, i : i + 1],
                base_ref[1, 0, :, i : i + 1],
            )
            part[i] = both[:k1_count] + both[k1_count:] - base
        at = pl.multiple_of(step * CHUNK, CHUNK)
        turned_high, turned_low = split(jnp.swapaxes(part[...], 0, 1))
        middle[:, pl.ds(at, CHUNK), :] = turned_high
        middle[:, pl.ds(k0_count + at, CHUNK), :] = turned_low

    @pl.when(step >= steps)
    def _():
        first = (step - steps) * CHUNK
        for i in range(0, CHUNK, 2):
            at = first + i
            columns = jnp.concatenate((middle[at], middle[at + 1]), axis=1)
            both = jnp.dot(fine_ref[...], columns, preferred_element_type=jnp.float32)
            half = both.shape[0] // 2
            both = both[:half] + both[half:]
            by_real, by_imag = both[: half // 2], both[half // 2 :]
            for j in range(2):
                own = slice(j * lanes, (j + 1) * lanes)
                part[i + j] = by_real[:, own] + sign * swap_halves(by_imag[:, own])
        turned = jnp.swapaxes(part[...], 0, 1).astype(jnp.bfloat16)
        out_ref[...] = turned.reshape(out_ref.shape)


def depth_transform(me, pieces, matrices, base, devices):
    wave_count = len(pieces)
    k1_part, k0_count, lanes = pieces[0].shape
    k1_count = wave_count * k1_part
    length = k1_count * k0_count
    steps = k0_count // CHUNK
    fine = np.concatenate(unit_roots(k0_count, k0_count, k0_count), axis=0) / math.sqrt(length)
    fine_high = fine.astype(jnp.bfloat16)
    fine_low = (fine - fine_high.astype(np.float64)).astype(jnp.bfloat16)
    fine = np.concatenate((fine_high, fine_low), axis=0)
    fine = np.concatenate((fine, fine), axis=1)
    out_shape = (devices, k0_count // devices, k1_count, lanes)
    return pl.pallas_call(
        functools.partial(transform_kernel, steps),
        out_shape=jax.ShapeDtypeStruct(out_shape, jnp.bfloat16),
        grid=(2 * steps,),
        in_specs=[pl.BlockSpec(memory_space=pltpu.SMEM)]
        + [
            pl.BlockSpec((k1_part, CHUNK, lanes), lambda i: (0, jnp.minimum(i, steps - 1), 0))
        ]
        * wave_count
        + [
            pl.BlockSpec(
                (CHUNK, 2 * k1_count, 2 * k1_count), lambda i: (jnp.minimum(i, steps - 1), 0, 0)
            ),
            pl.BlockSpec(
                (2, 1, k1_count, CHUNK), lambda i: (0, jnp.minimum(i, steps - 1), 0, 0)
            ),
            pl.BlockSpec(fine.shape, lambda i: (0, 0)),
        ],
        out_specs=pl.BlockSpec(
            out_shape[:2] + (CHUNK, lanes), lambda i: (0, 0, jnp.maximum(i - steps, 0), 0)
        ),
        scratch_shapes=[
            pltpu.VMEM((CHUNK, 2 * k1_count, lanes), jnp.bfloat16),
            pltpu.VMEM((k1_count, 2 * k0_count, lanes), jnp.bfloat16),
            pltpu.VMEM((CHUNK, k1_count, lanes), jnp.float32),
        ],
        compiler_params=pltpu.CompilerParams(vmem_limit_bytes=VMEM_BYTES),
        cost_estimate=pl.CostEstimate(
            flops=MATRIX_COST, bytes_accessed=12 * length * lanes, transcendentals=0
        ),
    )(me, *pieces, matrices, base, jnp.asarray(fine))


def even_masks(count):
    return [mask for mask in range(count) if bin(mask).count("1") % 2 == 0]


def refocus_kernel(wave_count, pix_count, me_ref, depth_ref, *refs):
    prop_refs = refs[: 2 * wave_count]
    out_ref, rows = refs[-2:]
    _, depths, lanes = depth_ref.shape
    half = pix_count // 2
    core = me_ref[1]

    @pl.when(pl.program_id(0) == 0)
    def _():
        sign = jnp.where(left_half((1, lanes)), 1.0, -1.0)
        for m in range(wave_count):
            first = (me_ref[0] ^ m) * pix_count
            for h in range(2):
                start = first + (h if m in even_masks(wave_count) else core ^ h) * half
                for p in range(half):
                    at = (m * pix_count + h * half + p) * lanes
                    own = slice(at, at + lanes)
                    value = depth_ref[start + p].astype(jnp.float32)
                    rows[:depths, own] = (value * sign).astype(jnp.bfloat16)
                    rows[depths:, own] = swap_halves(value).astype(jnp.bfloat16)

    columns = jnp.concatenate(
        [ref[...].reshape(half * lanes, ref.shape[-1]) for ref in prop_refs], axis=0
    )
    for c in range(2):
        out_ref[c, 0] = jnp.dot(
            rows[c * depths : (c + 1) * depths], columns, preferred_element_type=jnp.float32
        )


def refocus(me, depth, gathered, fetched, row, row_count, image):
    wave_count = 2 * gathered.shape[1]
    senders, depths, lanes = depth.shape
    pix_count = senders // wave_count
    span = pix_count // 2 * lanes
    columns = gathered.shape[3]
    even = even_masks(wave_count)
    operands, specs = [], []
    for mask in range(wave_count):
        for h in range(2):
            if mask in even:
                at = even.index(mask)
                operands.append(gathered)
                specs.append(
                    pl.BlockSpec((1, 1, span, columns), lambda q, at=at, h=h: (q, at, h, 0))
                )
            else:
                operands.append(fetched[mask][h])
                specs.append(pl.BlockSpec((1, span, columns), lambda q: (q, 0, 0)))
    earlier = () if image is None else (image,)
    return pl.pallas_call(
        functools.partial(refocus_kernel, wave_count, pix_count),
        out_shape=jax.ShapeDtypeStruct(
            (2, row_count, depths, pix_count * columns), jnp.float32
        ),
        grid=(pix_count,),
        in_specs=[
            pl.BlockSpec(memory_space=pltpu.SMEM),
            pl.BlockSpec(depth.shape, lambda q: (0, 0, 0)),
        ]
        + specs
        + [pl.BlockSpec(memory_space=pl.ANY)] * len(earlier),
        out_specs=pl.BlockSpec((2, 1, depths, columns), lambda q: (0, row, 0, q)),
        input_output_aliases={2 + len(operands): 0} if earlier else {},
        scratch_shapes=[pltpu.VMEM((2 * depths, senders * lanes), jnp.bfloat16)],
        compiler_params=pltpu.CompilerParams(vmem_limit_bytes=VMEM_BYTES),
        cost_estimate=pl.CostEstimate(
            flops=MATRIX_COST,
            bytes_accessed=28 * 1024 * 1024,
            transcendentals=0,
        ),
    )(me, depth, *operands, *earlier)


def own_slices(propagator, wave_pos, wave_count):
    _, span, pix_local = propagator.shape
    rows = propagator.reshape(2, lax.axis_size("pix"), wave_count, -1, pix_local)
    slices = []
    for mask in even_masks(wave_count):
        own = lax.dynamic_index_in_dim(rows, wave_pos ^ mask, axis=2, keepdims=False)
        slices.append(jnp.swapaxes(own, 0, 1).reshape(2 * span // wave_count, pix_local))
    return jnp.stack(slices)


def exchange_slices(gathered, wave_count, core):
    pix_count, _, span, columns = gathered.shape
    half = span // 2
    result = {}
    for mask in range(wave_count):
        if mask not in even_masks(wave_count):
            bit = mask & -mask
            at = even_masks(wave_count).index(mask ^ bit)
            own = lax.dynamic_slice(
                gathered, (0, at, core * half, 0), (pix_count, 1, half, columns)
            ).reshape(pix_count, half, columns)
            own = lax.ppermute(own, "wave", [(s, s ^ bit) for s in range(wave_count)])
            mate = lax.ppermute(own, "pix", [(s, s ^ 1) for s in range(pix_count)])
            result[mask] = (own, mate)
    return result


def on_device(raw_spectra, background, dispersion, propagator):
    _, row_count, wave_span, pix_local = raw_spectra.shape
    wave_count = lax.axis_size("wave")
    pix_count = lax.axis_size("pix")
    devices = wave_count * pix_count
    pixels = pix_local // wave_count
    k0_count = 128
    k1_part = wave_span // k0_count
    k1_count = k1_part * wave_count
    wave_pos = lax.axis_index("wave")
    core = lax.axis_index("pix") % 2
    me = jnp.stack((wave_pos, core)).astype(jnp.int32)
    own = own_slices(propagator, wave_pos, wave_count)
    own, me = lax.optimization_barrier((own, me))
    gathered = lax.all_gather(own, "pix", axis=0, tiled=False)

    phases = jnp.stack((jnp.cos(dispersion), jnp.sin(dispersion), background))
    phases = phases.reshape(1, 3, k1_part, k0_count)
    phases = jnp.broadcast_to(phases, (wave_count,) + phases.shape[1:])
    phases = lax.all_to_all(phases, "wave", split_axis=0, concat_axis=0, tiled=True)
    phases = jnp.transpose(phases, (1, 3, 0, 2)).reshape(3, k0_count, k1_count)

    raw = raw_spectra.reshape(2, row_count, k1_part, k0_count, pix_local)
    packed = [pack(me, raw, wave_count, row) for row in range(row_count)]
    packed[0], phases = lax.optimization_barrier((packed[0], phases))
    matrices, base = stage_matrices(phases)
    image = None
    for row in range(row_count):
        arrived = [packed[row][0]] + [
            lax.ppermute(packed[row][m], "wave", [(s, s ^ m) for s in range(wave_count)])
            for m in range(1, wave_count)
        ]
        if row + 1 < row_count:
            arrived, packed[row + 1] = lax.optimization_barrier((arrived, packed[row + 1]))
        if row == 0:
            fetched = exchange_slices(gathered, wave_count, core)
        depth = depth_transform(me, arrived, matrices, base, devices)
        depth = depth.reshape(devices, -1, 2 * pixels)
        depth = lax.all_to_all(depth, ("wave", "pix"), split_axis=0, concat_axis=0, tiled=True)
        image = refocus(me, depth, gathered, fetched, row, row_count, image)
    return image


def solution(mesh):
    in_specs = (P(None, None, "wave", "pix"), P("wave"), P("wave"), P(None, None, "pix"))
    out_specs = P(None, None, ("wave", "pix"), None)
    return jax.shard_map(
        on_device, mesh=mesh, in_specs=in_specs, out_specs=out_specs, check_vma=False
    )
```

```python
import functools
import math

import jax
import jax.numpy as jnp
import numpy as np
from jax import lax
from jax.experimental import pallas as pl
from jax.experimental.pallas import tpu as pltpu
from jax.sharding import PartitionSpec as P

CHUNK = 16
MATRIX_COST = 120 * 10**9
VMEM_BYTES = 56 * 1024 * 1024


def unit_roots(rows, columns, modulus):
    product = np.outer(np.arange(rows), np.arange(columns)) % modulus
    angle = -2.0 * np.pi / modulus * product
    return np.cos(angle), np.sin(angle)


def split(value):
    high = value.astype(jnp.bfloat16)
    return high, (value - high.astype(jnp.float32)).astype(jnp.bfloat16)


def swap_halves(value):
    half = value.shape[-1] // 2
    if 2 * half == 128:
        return pltpu.roll(value, half, value.ndim - 1)
    return jnp.concatenate((value[..., half:], value[..., :half]), axis=-1)


def left_half(shape):
    return lax.broadcasted_iota(jnp.int32, shape, len(shape) - 1) < shape[-1] // 2


def pack_kernel(me_ref, raw_ref, *out_refs):
    count = len(out_refs)
    pixels = out_refs[0].shape[2] // 2
    for me in range(count):

        @pl.when(me_ref[0] == me)
        def _():
            for m in range(count):
                lanes = slice((me ^ m) * pixels, (me ^ m) * pixels + pixels)
                parts = (raw_ref[0, 0, :, :, lanes], raw_ref[1, 0, :, :, lanes])
                out_refs[m][...] = jnp.concatenate(parts, axis=2)


def pack(me, raw, wave_count, row):
    _, _, k1_part, k0_count, pix_local = raw.shape
    lanes = 2 * pix_local // wave_count
    span = min(4, k1_part)
    return pl.pallas_call(
        pack_kernel,
        out_shape=[jax.ShapeDtypeStruct((k1_part, k0_count, lanes), raw.dtype)] * wave_count,
        grid=(k1_part // span,),
        in_specs=[
            pl.BlockSpec(memory_space=pltpu.SMEM),
            pl.BlockSpec((2, 1, span, k0_count, pix_local), lambda k: (0, row, k, 0, 0)),
        ],
        out_specs=[pl.BlockSpec((span, k0_count, lanes), lambda k: (k, 0, 0))] * wave_count,
        compiler_params=pltpu.CompilerParams(vmem_limit_bytes=VMEM_BYTES),
        cost_estimate=pl.CostEstimate(
            flops=0, bytes_accessed=8 * k1_part * k0_count * pix_local, transcendentals=0
        ),
    )(me, raw)


def matrix_kernel(phase_ref, small_ref, turn_ref, matrix_ref, base_ref):
    bases = []
    for i in range(CHUNK):
        turn_real = turn_ref[0, 0, :, i : i + 1]
        turn_imag = turn_ref[1, 0, :, i : i + 1]
        cosine = phase_ref[0, i : i + 1, :]
        sine = phase_ref[1, i : i + 1, :]
        background = phase_ref[2, i : i + 1, :]
        small_real = small_ref[0] * turn_real - small_ref[1] * turn_imag
        small_imag = small_ref[0] * turn_imag + small_ref[1] * turn_real
        real = small_real * cosine - small_imag * sine
        imag = small_real * sine + small_imag * cosine
        bases.append([jnp.sum(v * background, axis=1, keepdims=True) for v in (real, imag)])
        real_high, real_low = split(real)
        imag_high, imag_low = split(imag)
        count = real.shape[0]
        matrix_ref[i, :count] = jnp.concatenate((real_high, imag_high), axis=1)
        matrix_ref[i, count:] = jnp.concatenate((real_low, imag_low), axis=1)
    for c in range(2):
        base_ref[c, 0] = jnp.concatenate([base[c] for base in bases], axis=1)


def stage_matrices(phases):
    _, k0_count, k1_count = phases.shape
    length = k1_count * k0_count
    steps = k0_count // CHUNK
    small = np.stack(unit_roots(k1_count, k1_count, k1_count)).astype(np.float32)
    turn = np.stack(unit_roots(k1_count, k0_count, length)).astype(np.float32)
    turn = turn.reshape(2, k1_count, steps, CHUNK).transpose(0, 2, 1, 3)
    column_spec = pl.BlockSpec((2, 1, k1_count, CHUNK), lambda i: (0, i, 0, 0))
    return pl.pallas_call(
        matrix_kernel,
        out_shape=(
            jax.ShapeDtypeStruct((k0_count, 2 * k1_count, 2 * k1_count), jnp.bfloat16),
            jax.ShapeDtypeStruct((2, steps, k1_count, CHUNK), jnp.float32),
        ),
        grid=(steps,),
        in_specs=[
            pl.BlockSpec((3, CHUNK, k1_count), lambda i: (0, i, 0)),
            pl.BlockSpec(small.shape, lambda i: (0, 0, 0)),
            column_spec,
        ],
        out_specs=(
            pl.BlockSpec((CHUNK, 2 * k1_count, 2 * k1_count), lambda i: (i, 0, 0)),
            column_spec,
        ),
        compiler_params=pltpu.CompilerParams(vmem_limit_bytes=VMEM_BYTES),
        cost_estimate=pl.CostEstimate(
            flops=20 * length * k1_count, bytes_accessed=8 * length * k1_count, transcendentals=0
        ),
    )(phases, jnp.asarray(small), jnp.asarray(turn))


def transform_kernel(steps, me_ref, *refs):
    x_refs = refs[:-7]
    matrix_ref, base_ref, fine_ref, out_ref, data, middle, part = refs[-7:]
    step = pl.program_id(0)
    k1_count, lanes = data.shape[1] // 2, data.shape[2]
    k0_count = middle.shape[1] // 2
    k1_part = x_refs[0].shape[0]
    sign = jnp.where(left_half((1, lanes)), -1.0, 1.0)

    @pl.when(step < steps)
    def _():
        for m, x_ref in enumerate(x_refs):
            start = pl.multiple_of((me_ref[0] ^ m) * k1_part, k1_part)
            block = jnp.swapaxes(x_ref[...].astype(jnp.float32), 0, 1)
            data[:, pl.ds(start, k1_part), :] = block.astype(jnp.bfloat16)
            other = swap_halves(block) * sign
            data[:, pl.ds(k1_count + start, k1_part), :] = other.astype(jnp.bfloat16)
        for i in range(CHUNK):
            both = jnp.dot(matrix_ref[i], data[i], preferred_element_type=jnp.float32)
            base = jnp.where(
                left_half((k1_count, lanes)),
                base_ref[0, 0, :, i : i + 1],
                base_ref[1, 0, :, i : i + 1],
            )
            part[i] = both[:k1_count] + both[k1_count:] - base
        at = pl.multiple_of(step * CHUNK, CHUNK)
        turned_high, turned_low = split(jnp.swapaxes(part[...], 0, 1))
        middle[:, pl.ds(at, CHUNK), :] = turned_high
        middle[:, pl.ds(k0_count + at, CHUNK), :] = turned_low

    @pl.when(step >= steps)
    def _():
        first = (step - steps) * CHUNK
        for i in range(0, CHUNK, 2):
            at = first + i
            columns = jnp.concatenate((middle[at], middle[at + 1]), axis=1)
            both = jnp.dot(fine_ref[...], columns, preferred_element_type=jnp.float32)
            half = both.shape[0] // 2
            both = both[:half] + both[half:]
            by_real, by_imag = both[: half // 2], both[half // 2 :]
            for j in range(2):
                own = slice(j * lanes, (j + 1) * lanes)
                part[i + j] = by_real[:, own] + sign * swap_halves(by_imag[:, own])
        turned = jnp.swapaxes(part[...], 0, 1).astype(jnp.bfloat16)
        out_ref[...] = turned.reshape(out_ref.shape)


def depth_transform(me, pieces, matrices, base, devices):
    wave_count = len(pieces)
    k1_part, k0_count, lanes = pieces[0].shape
    k1_count = wave_count * k1_part
    length = k1_count * k0_count
    steps = k0_count // CHUNK
    fine = np.concatenate(unit_roots(k0_count, k0_count, k0_count), axis=0) / math.sqrt(length)
    fine_high = fine.astype(jnp.bfloat16)
    fine_low = (fine - fine_high.astype(np.float64)).astype(jnp.bfloat16)
    fine = np.concatenate((fine_high, fine_low), axis=0)
    fine = np.concatenate((fine, fine), axis=1)
    out_shape = (devices, k0_count // devices, k1_count, lanes)
    return pl.pallas_call(
        functools.partial(transform_kernel, steps),
        out_shape=jax.ShapeDtypeStruct(out_shape, jnp.bfloat16),
        grid=(2 * steps,),
        in_specs=[pl.BlockSpec(memory_space=pltpu.SMEM)]
        + [
            pl.BlockSpec((k1_part, CHUNK, lanes), lambda i: (0, jnp.minimum(i, steps - 1), 0))
        ]
        * wave_count
        + [
            pl.BlockSpec(
                (CHUNK, 2 * k1_count, 2 * k1_count), lambda i: (jnp.minimum(i, steps - 1), 0, 0)
            ),
            pl.BlockSpec(
                (2, 1, k1_count, CHUNK), lambda i: (0, jnp.minimum(i, steps - 1), 0, 0)
            ),
            pl.BlockSpec(fine.shape, lambda i: (0, 0)),
        ],
        out_specs=pl.BlockSpec(
            out_shape[:2] + (CHUNK, lanes), lambda i: (0, 0, jnp.maximum(i - steps, 0), 0)
        ),
        scratch_shapes=[
            pltpu.VMEM((CHUNK, 2 * k1_count, lanes), jnp.bfloat16),
            pltpu.VMEM((k1_count, 2 * k0_count, lanes), jnp.bfloat16),
            pltpu.VMEM((CHUNK, k1_count, lanes), jnp.float32),
        ],
        compiler_params=pltpu.CompilerParams(vmem_limit_bytes=VMEM_BYTES),
        cost_estimate=pl.CostEstimate(
            flops=MATRIX_COST, bytes_accessed=12 * length * lanes, transcendentals=0
        ),
    )(me, *pieces, matrices, base, jnp.asarray(fine))


def even_masks(count):
    return [mask for mask in range(count) if bin(mask).count("1") % 2 == 0]


def refocus_kernel(wave_count, pix_count, me_ref, depth_ref, *refs):
    prop_refs = refs[: 2 * wave_count]
    out_ref, rows = refs[-2:]
    _, depths, lanes = depth_ref.shape
    half = pix_count // 2
    core = me_ref[1]

    @pl.when(pl.program_id(0) == 0)
    def _():
        sign = jnp.where(left_half((1, lanes)), 1.0, -1.0)
        for m in range(wave_count):
            first = (me_ref[0] ^ m) * pix_count
            for h in range(2):
                start = first + (h if m in even_masks(wave_count) else core ^ h) * half
                for p in range(half):
                    at = (m * pix_count + h * half + p) * lanes
                    own = slice(at, at + lanes)
                    value = depth_ref[start + p].astype(jnp.float32)
                    rows[:depths, own] = (value * sign).astype(jnp.bfloat16)
                    rows[depths:, own] = swap_halves(value).astype(jnp.bfloat16)

    columns = jnp.concatenate(
        [ref[...].reshape(half * lanes, ref.shape[-1]) for ref in prop_refs], axis=0
    )
    for c in range(2):
        out_ref[c, 0] = jnp.dot(
            rows[c * depths : (c + 1) * depths], columns, preferred_element_type=jnp.float32
        )


def refocus(me, depth, gathered, fetched, row, row_count, image):
    wave_count = 2 * gathered.shape[1]
    senders, depths, lanes = depth.shape
    pix_count = senders // wave_count
    span = pix_count // 2 * lanes
    columns = gathered.shape[3]
    even = even_masks(wave_count)
    operands, specs = [], []
    for mask in range(wave_count):
        for h in range(2):
            if mask in even:
                at = even.index(mask)
                operands.append(gathered)
                specs.append(
                    pl.BlockSpec((1, 1, span, columns), lambda q, at=at, h=h: (q, at, h, 0))
                )
            else:
                operands.append(fetched[mask][h])
                specs.append(pl.BlockSpec((1, span, columns), lambda q: (q, 0, 0)))
    earlier = () if image is None else (image,)
    return pl.pallas_call(
        functools.partial(refocus_kernel, wave_count, pix_count),
        out_shape=jax.ShapeDtypeStruct(
            (2, row_count, depths, pix_count * columns), jnp.float32
        ),
        grid=(pix_count,),
        in_specs=[
            pl.BlockSpec(memory_space=pltpu.SMEM),
            pl.BlockSpec(depth.shape, lambda q: (0, 0, 0)),
        ]
        + specs
        + [pl.BlockSpec(memory_space=pl.ANY)] * len(earlier),
        out_specs=pl.BlockSpec((2, 1, depths, columns), lambda q: (0, row, 0, q)),
        input_output_aliases={2 + len(operands): 0} if earlier else {},
        scratch_shapes=[pltpu.VMEM((2 * depths, senders * lanes), jnp.bfloat16)],
        compiler_params=pltpu.CompilerParams(vmem_limit_bytes=VMEM_BYTES),
        cost_estimate=pl.CostEstimate(
            flops=MATRIX_COST,
            bytes_accessed=28 * 1024 * 1024,
            transcendentals=0,
        ),
    )(me, depth, *operands, *earlier)


def own_slices(propagator, wave_pos, wave_count):
    _, span, pix_local = propagator.shape
    rows = propagator.reshape(2, lax.axis_size("pix"), wave_count, -1, pix_local)
    slices = []
    for mask in even_masks(wave_count):
        own = lax.dynamic_index_in_dim(rows, wave_pos ^ mask, axis=2, keepdims=False)
        slices.append(jnp.swapaxes(own, 0, 1).reshape(2 * span // wave_count, pix_local))
    return jnp.stack(slices)


def fetch_slices(gathered, wave_count, core):
    pix_count, _, span, columns = gathered.shape
    half = span // 2
    fetched = {}
    for mask in range(wave_count):
        if mask not in even_masks(wave_count):
            bit = mask & -mask
            at = even_masks(wave_count).index(mask ^ bit)
            own = lax.dynamic_slice(
                gathered, (0, at, core * half, 0), (pix_count, 1, half, columns)
            ).reshape(pix_count, half, columns)
            fetched[mask] = lax.ppermute(
                own, "wave", [(s, s ^ bit) for s in range(wave_count)]
            )
    return fetched


def swap_cores(fetched):
    pairs = [(s, s ^ 1) for s in range(lax.axis_size("pix"))]
    return {mask: (own, lax.ppermute(own, "pix", pairs)) for mask, own in fetched.items()}


def on_device(raw_spectra, background, dispersion, propagator):
    _, row_count, wave_span, pix_local = raw_spectra.shape
    wave_count = lax.axis_size("wave")
    pix_count = lax.axis_size("pix")
    devices = wave_count * pix_count
    pixels = pix_local // wave_count
    k0_count = 128
    k1_part = wave_span // k0_count
    k1_count = k1_part * wave_count
    wave_pos = lax.axis_index("wave")
    core = lax.axis_index("pix") % 2
    me = jnp.stack((wave_pos, core)).astype(jnp.int32)
    own = own_slices(propagator, wave_pos, wave_count)
    own, me = lax.optimization_barrier((own, me))
    gathered = lax.all_gather(own, "pix", axis=0, tiled=False)

    phases = jnp.stack((jnp.cos(dispersion), jnp.sin(dispersion), background))
    phases = phases.reshape(1, 3, k1_part, k0_count)
    phases = jnp.broadcast_to(phases, (wave_count,) + phases.shape[1:])
    phases = lax.all_to_all(phases, "wave", split_axis=0, concat_axis=0, tiled=True)
    phases = jnp.transpose(phases, (1, 3, 0, 2)).reshape(3, k0_count, k1_count)

    raw = raw_spectra.reshape(2, row_count, k1_part, k0_count, pix_local)
    packed = [pack(me, raw, wave_count, row) for row in range(row_count)]
    packed[0], phases = lax.optimization_barrier((packed[0], phases))
    matrices, base = stage_matrices(phases)
    depths = []
    for row in range(row_count):
        arrived = [packed[row][0]] + [
            lax.ppermute(packed[row][m], "wave", [(s, s ^ m) for s in range(wave_count)])
            for m in range(1, wave_count)
        ]
        if row + 1 < row_count:
            arrived, packed[row + 1] = lax.optimization_barrier((arrived, packed[row + 1]))
        depth = depth_transform(me, arrived, matrices, base, devices)
        if row == 0:
            source, _ = lax.optimization_barrier((gathered, depth))
            fetched = fetch_slices(source, wave_count, core)
        if row == row_count - 1:
            fetched, _ = lax.optimization_barrier((fetched, depth))
            fetched = swap_cores(fetched)
        depth = depth.reshape(devices, -1, 2 * pixels)
        depth = lax.all_to_all(depth, ("wave", "pix"), split_axis=0, concat_axis=0, tiled=True)
        depths.append(depth)
    image = None
    for row, depth in enumerate(depths):
        image = refocus(me, depth, gathered, fetched, row, row_count, image)
    return image


def solution(mesh):
    in_specs = (P(None, None, "wave", "pix"), P("wave"), P("wave"), P(None, None, "pix"))
    out_specs = P(None, None, ("wave", "pix"), None)
    return jax.shard_map(
        on_device, mesh=mesh, in_specs=in_specs, out_specs=out_specs, check_vma=False
    )
```

```python
import functools
import math

import jax
import jax.numpy as jnp
import numpy as np
from jax import lax
from jax.experimental import pallas as pl
from jax.experimental.pallas import tpu as pltpu
from jax.sharding import PartitionSpec as P

CHUNK = 16
MATRIX_COST = 120 * 10**9
VMEM_BYTES = 56 * 1024 * 1024


def unit_roots(rows, columns, modulus):
    product = np.outer(np.arange(rows), np.arange(columns)) % modulus
    angle = -2.0 * np.pi / modulus * product
    return np.cos(angle), np.sin(angle)


def split(value):
    high = value.astype(jnp.bfloat16)
    return high, (value - high.astype(jnp.float32)).astype(jnp.bfloat16)


def swap_halves(value):
    half = value.shape[-1] // 2
    if 2 * half == 128:
        return pltpu.roll(value, half, value.ndim - 1)
    return jnp.concatenate((value[..., half:], value[..., :half]), axis=-1)


def left_half(shape):
    return lax.broadcasted_iota(jnp.int32, shape, len(shape) - 1) < shape[-1] // 2


def pack_kernel(me_ref, raw_ref, *out_refs):
    count = len(out_refs)
    pixels = out_refs[0].shape[2] // 2
    for me in range(count):

        @pl.when(me_ref[0] == me)
        def _():
            for m in range(count):
                lanes = slice((me ^ m) * pixels, (me ^ m) * pixels + pixels)
                parts = (raw_ref[0, 0, :, :, lanes], raw_ref[1, 0, :, :, lanes])
                out_refs[m][...] = jnp.concatenate(parts, axis=2)


def pack(me, raw, wave_count, row):
    _, _, k1_part, k0_count, pix_local = raw.shape
    lanes = 2 * pix_local // wave_count
    span = min(4, k1_part)
    return pl.pallas_call(
        pack_kernel,
        out_shape=[jax.ShapeDtypeStruct((k1_part, k0_count, lanes), raw.dtype)] * wave_count,
        grid=(k1_part // span,),
        in_specs=[
            pl.BlockSpec(memory_space=pltpu.SMEM),
            pl.BlockSpec((2, 1, span, k0_count, pix_local), lambda k: (0, row, k, 0, 0)),
        ],
        out_specs=[pl.BlockSpec((span, k0_count, lanes), lambda k: (k, 0, 0))] * wave_count,
        compiler_params=pltpu.CompilerParams(vmem_limit_bytes=VMEM_BYTES),
        cost_estimate=pl.CostEstimate(
            flops=0, bytes_accessed=8 * k1_part * k0_count * pix_local, transcendentals=0
        ),
    )(me, raw)


def matrix_kernel(phase_ref, small_ref, turn_ref, matrix_ref, base_ref):
    bases = []
    for i in range(CHUNK):
        turn_real = turn_ref[0, 0, :, i : i + 1]
        turn_imag = turn_ref[1, 0, :, i : i + 1]
        cosine = phase_ref[0, i : i + 1, :]
        sine = phase_ref[1, i : i + 1, :]
        background = phase_ref[2, i : i + 1, :]
        small_real = small_ref[0] * turn_real - small_ref[1] * turn_imag
        small_imag = small_ref[0] * turn_imag + small_ref[1] * turn_real
        real = small_real * cosine - small_imag * sine
        imag = small_real * sine + small_imag * cosine
        bases.append([jnp.sum(v * background, axis=1, keepdims=True) for v in (real, imag)])
        real_high, real_low = split(real)
        imag_high, imag_low = split(imag)
        count = real.shape[0]
        matrix_ref[i, :count] = jnp.concatenate((real_high, imag_high), axis=1)
        matrix_ref[i, count:] = jnp.concatenate((real_low, imag_low), axis=1)
    for c in range(2):
        base_ref[c, 0] = jnp.concatenate([base[c] for base in bases], axis=1)


def stage_matrices(phases):
    _, k0_count, k1_count = phases.shape
    length = k1_count * k0_count
    steps = k0_count // CHUNK
    small = np.stack(unit_roots(k1_count, k1_count, k1_count)).astype(np.float32)
    turn = np.stack(unit_roots(k1_count, k0_count, length)).astype(np.float32)
    turn = turn.reshape(2, k1_count, steps, CHUNK).transpose(0, 2, 1, 3)
    column_spec = pl.BlockSpec((2, 1, k1_count, CHUNK), lambda i: (0, i, 0, 0))
    return pl.pallas_call(
        matrix_kernel,
        out_shape=(
            jax.ShapeDtypeStruct((k0_count, 2 * k1_count, 2 * k1_count), jnp.bfloat16),
            jax.ShapeDtypeStruct((2, steps, k1_count, CHUNK), jnp.float32),
        ),
        grid=(steps,),
        in_specs=[
            pl.BlockSpec((3, CHUNK, k1_count), lambda i: (0, i, 0)),
            pl.BlockSpec(small.shape, lambda i: (0, 0, 0)),
            column_spec,
        ],
        out_specs=(
            pl.BlockSpec((CHUNK, 2 * k1_count, 2 * k1_count), lambda i: (i, 0, 0)),
            column_spec,
        ),
        compiler_params=pltpu.CompilerParams(vmem_limit_bytes=VMEM_BYTES),
        cost_estimate=pl.CostEstimate(
            flops=20 * length * k1_count, bytes_accessed=8 * length * k1_count, transcendentals=0
        ),
    )(phases, jnp.asarray(small), jnp.asarray(turn))


def transform_kernel(steps, me_ref, *refs):
    x_refs = refs[:-7]
    matrix_ref, base_ref, fine_ref, out_ref, data, middle, part = refs[-7:]
    step = pl.program_id(0)
    k1_count, lanes = data.shape[1] // 2, data.shape[2]
    k0_count = middle.shape[1] // 2
    k1_part = x_refs[0].shape[0]
    sign = jnp.where(left_half((1, lanes)), -1.0, 1.0)

    @pl.when(step < steps)
    def _():
        for m, x_ref in enumerate(x_refs):
            start = pl.multiple_of((me_ref[0] ^ m) * k1_part, k1_part)
            block = jnp.swapaxes(x_ref[...].astype(jnp.float32), 0, 1)
            data[:, pl.ds(start, k1_part), :] = block.astype(jnp.bfloat16)
            other = swap_halves(block) * sign
            data[:, pl.ds(k1_count + start, k1_part), :] = other.astype(jnp.bfloat16)
        for i in range(CHUNK):
            both = jnp.dot(matrix_ref[i], data[i], preferred_element_type=jnp.float32)
            base = jnp.where(
                left_half((k1_count, lanes)),
                base_ref[0, 0, :, i : i + 1],
                base_ref[1, 0, :, i : i + 1],
            )
            part[i] = both[:k1_count] + both[k1_count:] - base
        at = pl.multiple_of(step * CHUNK, CHUNK)
        turned_high, turned_low = split(jnp.swapaxes(part[...], 0, 1))
        middle[:, pl.ds(at, CHUNK), :] = turned_high
        middle[:, pl.ds(k0_count + at, CHUNK), :] = turned_low

    @pl.when(step >= steps)
    def _():
        first = (step - steps) * CHUNK
        for i in range(0, CHUNK, 2):
            at = first + i
            columns = jnp.concatenate((middle[at], middle[at + 1]), axis=1)
            both = jnp.dot(fine_ref[...], columns, preferred_element_type=jnp.float32)
            half = both.shape[0] // 2
            both = both[:half] + both[half:]
            by_real, by_imag = both[: half // 2], both[half // 2 :]
            for j in range(2):
                own = slice(j * lanes, (j + 1) * lanes)
                part[i + j] = by_real[:, own] + sign * swap_halves(by_imag[:, own])
        turned = jnp.swapaxes(part[...], 0, 1).astype(jnp.bfloat16)
        out_ref[...] = turned.reshape(out_ref.shape)


def depth_transform(me, pieces, matrices, base, devices):
    wave_count = len(pieces)
    k1_part, k0_count, lanes = pieces[0].shape
    k1_count = wave_count * k1_part
    length = k1_count * k0_count
    steps = k0_count // CHUNK
    fine = np.concatenate(unit_roots(k0_count, k0_count, k0_count), axis=0) / math.sqrt(length)
    fine_high = fine.astype(jnp.bfloat16)
    fine_low = (fine - fine_high.astype(np.float64)).astype(jnp.bfloat16)
    fine = np.concatenate((fine_high, fine_low), axis=0)
    fine = np.concatenate((fine, fine), axis=1)
    out_shape = (devices, k0_count // devices, k1_count, lanes)
    return pl.pallas_call(
        functools.partial(transform_kernel, steps),
        out_shape=jax.ShapeDtypeStruct(out_shape, jnp.bfloat16),
        grid=(2 * steps,),
        in_specs=[pl.BlockSpec(memory_space=pltpu.SMEM)]
        + [
            pl.BlockSpec((k1_part, CHUNK, lanes), lambda i: (0, jnp.minimum(i, steps - 1), 0))
        ]
        * wave_count
        + [
            pl.BlockSpec(
                (CHUNK, 2 * k1_count, 2 * k1_count), lambda i: (jnp.minimum(i, steps - 1), 0, 0)
            ),
            pl.BlockSpec(
                (2, 1, k1_count, CHUNK), lambda i: (0, jnp.minimum(i, steps - 1), 0, 0)
            ),
            pl.BlockSpec(fine.shape, lambda i: (0, 0)),
        ],
        out_specs=pl.BlockSpec(
            out_shape[:2] + (CHUNK, lanes), lambda i: (0, 0, jnp.maximum(i - steps, 0), 0)
        ),
        scratch_shapes=[
            pltpu.VMEM((CHUNK, 2 * k1_count, lanes), jnp.bfloat16),
            pltpu.VMEM((k1_count, 2 * k0_count, lanes), jnp.bfloat16),
            pltpu.VMEM((CHUNK, k1_count, lanes), jnp.float32),
        ],
        compiler_params=pltpu.CompilerParams(vmem_limit_bytes=VMEM_BYTES),
        cost_estimate=pl.CostEstimate(
            flops=MATRIX_COST, bytes_accessed=12 * length * lanes, transcendentals=0
        ),
    )(me, *pieces, matrices, base, jnp.asarray(fine))


def even_masks(count):
    return [mask for mask in range(count) if bin(mask).count("1") % 2 == 0]


def refocus_kernel(wave_count, pix_count, blocks, me_ref, depth_ref, *refs):
    prop_refs = refs[:blocks]
    out_ref, rows = refs[-2:]
    _, depths, lanes = depth_ref.shape
    half, quarter = pix_count // 2, pix_count // 4
    core = me_ref[1]

    @pl.when(pl.program_id(0) == 0)
    def _():
        sign = jnp.where(left_half((1, lanes)), 1.0, -1.0)
        for m in range(wave_count):
            first = (me_ref[0] ^ m) * pix_count
            for p in range(pix_count):
                source = first + p
                if m not in even_masks(wave_count) and p < half:
                    source = first + (core ^ (p // quarter)) * quarter + p % quarter
                at = (m * pix_count + p) * lanes
                own = slice(at, at + lanes)
                value = depth_ref[source].astype(jnp.float32)
                rows[:depths, own] = (value * sign).astype(jnp.bfloat16)
                rows[depths:, own] = swap_halves(value).astype(jnp.bfloat16)

    columns = jnp.concatenate(
        [ref[...].reshape(ref.shape[-2:]) for ref in prop_refs], axis=0
    )
    for c in range(2):
        out_ref[c, 0] = jnp.dot(
            rows[c * depths : (c + 1) * depths], columns, preferred_element_type=jnp.float32
        )


def refocus(me, depth, gathered, fetched, row, row_count, image):
    wave_count = 2 * gathered.shape[1]
    senders, depths, lanes = depth.shape
    pix_count = senders // wave_count
    span = pix_count // 2 * lanes
    columns = gathered.shape[3]
    even = even_masks(wave_count)
    operands, specs = [], []
    for mask in range(wave_count):
        if mask in even:
            at = even.index(mask)
            operands.append(gathered)
            specs.append(
                pl.BlockSpec((1, 1, 2 * span, columns), lambda q, at=at: (q, at, 0, 0))
            )
        else:
            for piece in fetched[mask]:
                operands.append(piece)
                specs.append(pl.BlockSpec((1,) + piece.shape[1:], lambda q: (q, 0, 0)))
    earlier = () if image is None else (image,)
    return pl.pallas_call(
        functools.partial(refocus_kernel, wave_count, pix_count, len(operands)),
        out_shape=jax.ShapeDtypeStruct(
            (2, row_count, depths, pix_count * columns), jnp.float32
        ),
        grid=(pix_count,),
        in_specs=[
            pl.BlockSpec(memory_space=pltpu.SMEM),
            pl.BlockSpec(depth.shape, lambda q: (0, 0, 0)),
        ]
        + specs
        + [pl.BlockSpec(memory_space=pl.ANY)] * len(earlier),
        out_specs=pl.BlockSpec((2, 1, depths, columns), lambda q: (0, row, 0, q)),
        input_output_aliases={2 + len(operands): 0} if earlier else {},
        scratch_shapes=[pltpu.VMEM((2 * depths, senders * lanes), jnp.bfloat16)],
        compiler_params=pltpu.CompilerParams(vmem_limit_bytes=VMEM_BYTES),
        cost_estimate=pl.CostEstimate(
            flops=MATRIX_COST,
            bytes_accessed=28 * 1024 * 1024,
            transcendentals=0,
        ),
    )(me, depth, *operands, *earlier)


def own_slices(propagator, wave_pos, wave_count):
    _, span, pix_local = propagator.shape
    rows = propagator.reshape(2, lax.axis_size("pix"), wave_count, -1, pix_local)
    slices = []
    for mask in even_masks(wave_count):
        own = lax.dynamic_index_in_dim(rows, wave_pos ^ mask, axis=2, keepdims=False)
        slices.append(jnp.swapaxes(own, 0, 1).reshape(2 * span // wave_count, pix_local))
    return jnp.stack(slices)


def fetch_slices(gathered, wave_count, start, rows):
    pix_count, _, _, columns = gathered.shape
    fetched = {}
    for mask in range(wave_count):
        if mask not in even_masks(wave_count):
            bit = mask & -mask
            at = even_masks(wave_count).index(mask ^ bit)
            own = lax.dynamic_slice(
                gathered, (0, at, start, 0), (pix_count, 1, rows, columns)
            ).reshape(pix_count, rows, columns)
            fetched[mask] = lax.ppermute(
                own, "wave", [(s, s ^ bit) for s in range(wave_count)]
            )
    return fetched


def swap_cores(value):
    return lax.ppermute(value, "pix", [(s, s ^ 1) for s in range(lax.axis_size("pix"))])


def on_device(raw_spectra, background, dispersion, propagator):
    _, row_count, wave_span, pix_local = raw_spectra.shape
    wave_count = lax.axis_size("wave")
    pix_count = lax.axis_size("pix")
    devices = wave_count * pix_count
    pixels = pix_local // wave_count
    k0_count = 128
    k1_part = wave_span // k0_count
    k1_count = k1_part * wave_count
    wave_pos = lax.axis_index("wave")
    core = lax.axis_index("pix") % 2
    me = jnp.stack((wave_pos, core)).astype(jnp.int32)
    own = own_slices(propagator, wave_pos, wave_count)
    own, me = lax.optimization_barrier((own, me))
    gathered = lax.all_gather(own, "pix", axis=0, tiled=False)

    phases = jnp.stack((jnp.cos(dispersion), jnp.sin(dispersion), background))
    phases = phases.reshape(1, 3, k1_part, k0_count)
    phases = jnp.broadcast_to(phases, (wave_count,) + phases.shape[1:])
    phases = lax.all_to_all(phases, "wave", split_axis=0, concat_axis=0, tiled=True)
    phases = jnp.transpose(phases, (1, 3, 0, 2)).reshape(3, k0_count, k1_count)

    raw = raw_spectra.reshape(2, row_count, k1_part, k0_count, pix_local)
    packed = [pack(me, raw, wave_count, row) for row in range(row_count)]
    packed[0], phases = lax.optimization_barrier((packed[0], phases))
    matrices, base = stage_matrices(phases)
    depths = []
    for row in range(row_count):
        arrived = [packed[row][0]] + [
            lax.ppermute(packed[row][m], "wave", [(s, s ^ m) for s in range(wave_count)])
            for m in range(1, wave_count)
        ]
        if row + 1 < row_count:
            arrived, packed[row + 1] = lax.optimization_barrier((arrived, packed[row + 1]))
        depth = depth_transform(me, arrived, matrices, base, devices)
        if row == 0:
            source, _ = lax.optimization_barrier((gathered, depth))
            quarter = source.shape[2] // 4
            shared = fetch_slices(source, wave_count, core * quarter, quarter)
        if row == row_count - 1:
            source, shared, _ = lax.optimization_barrier((source, shared, depth))
            whole = fetch_slices(source, wave_count, 2 * quarter, 2 * quarter)
            fetched = {m: (own, swap_cores(own), whole[m]) for m, own in shared.items()}
        depth = depth.reshape(devices, -1, 2 * pixels)
        depth = lax.all_to_all(depth, ("wave", "pix"), split_axis=0, concat_axis=0, tiled=True)
        depths.append(depth)
    image = None
    for row, depth in enumerate(depths):
        image = refocus(me, depth, gathered, fetched, row, row_count, image)
    return image


def solution(mesh):
    in_specs = (P(None, None, "wave", "pix"), P("wave"), P("wave"), P(None, None, "pix"))
    out_specs = P(None, None, ("wave", "pix"), None)
    return jax.shard_map(
        on_device, mesh=mesh, in_specs=in_specs, out_specs=out_specs, check_vma=False
    )
```
